32 devices in a mesh: expert: 8 (over z, x), tensor: 4 (over y, core).
Axes of the slice: x: 2, y: 2, z: 4, core: 2. Of those that a mesh axis runs over, the one named last changes fastest.
Arguments:
- tokens: bfloat16 [512, 1536], P('expert'), may hold values from -6 to 6
- exponents: int32 [512, 12], P('expert'), may hold values from -1 to 1
- out_grad: bfloat16 [512, 1536], P('expert'), may hold values from -6 to 6
- slots: int32 [8, 128], replicated, may hold values from 0 to 511, as said below
- gates: float32 [8, 128], P('expert'), may hold values from 0.1 to 1
- w_in: bfloat16 [8, 1536, 4096], P('expert', None, 'tensor'), may hold values from -0.15625 to 0.15625
- w_out: bfloat16 [8, 4096, 1536], P('expert', 'tensor'), may hold values from -0.09375 to 0.09375
Outputs:
- token_grad: bfloat16 [512, 1536], P(('expert', 'tensor'))
- w_in_grad: bfloat16 [8, 1536, 4096], P('expert', None, 'tensor')
- w_out_grad: bfloat16 [8, 4096, 1536], P('expert', 'tensor')
- gate_grad: float32 [8, 128], P('expert')
The draws below stay inside these ranges and needn't reach their ends.
Inputs may be any that keep to these rules, and one draw needn't show every extreme that they name: `slots`: each row holds 128 distinct token indices. In every row, at most 20 indices fall in any aligned block of 64 tokens (the tokens of one index of expert), and some block holds exactly 20.
All inputs are finite; a program needn't handle non-finite values.
Results may differ from the reference program's by a relative error of at most 0.007.
Values may be sent and summed in bfloat16 or wider, within the bound.
A program may use at most 64 MiB of HBM per device.

```python
import jax
import jax.numpy as jnp
from jax import lax

D = 1536
H = 4096
TOK_DEV = 64
E = 8
TOKENS = 512
C = 128
BLOCKS = 12


def row_perms(key, row_count, length):
    return jax.vmap(lambda sub_key: jax.random.permutation(sub_key, length))(jax.random.split(key, row_count))


def draw_slots(key, part):
    key = jax.random.fold_in(key, 11)
    key_shard, key_popular, key_jitter, key_order = jax.random.split(key, 4)
    average = C // E
    spread = C // (4 * E)
    shard_perm = row_perms(key_shard, E, E)
    shard_rank = jnp.argsort(shard_perm, axis=1)
    counts = jnp.where(shard_rank < E // 2, average + spread, average - spread)
    popular = jax.random.randint(key_popular, (TOKENS,), 0, 4)
    jitter = jax.random.randint(key_jitter, (E, TOKENS), 0, 8)
    within = jnp.arange(TOKENS) % TOK_DEV
    scores = (popular[None, :] * 8 + jitter) * TOK_DEV + within[None, :]
    scores = scores.reshape(E, E, TOK_DEV)
    ranking = jnp.argsort(-scores, axis=2)
    position = jnp.argsort(ranking, axis=2)
    picked = (position < counts[:, :, None]).reshape(E, TOKENS)
    chosen = jnp.argsort(jnp.where(picked, 0, 1), axis=1, stable=True)[:, :C]
    shuffle = row_perms(key_order, E, C)
    return jnp.take_along_axis(chosen, shuffle, axis=1).astype(jnp.int32)


def with_ends(array, own_key, smallest, top_value):
    longest = array.shape.index(max(array.shape))
    spots = []
    for shift in (0, 1):
        where = [jax.random.randint(jax.random.fold_in(own_key, axis), (), 0, length) for axis, length in enumerate(array.shape)]
        where[longest] = (where[longest] + shift) % array.shape[longest]
        spots.append(tuple(where))
    return array.at[spots[0]].set(smallest).at[spots[1]].set(top_value)


def steps_of(stream_key, dims, cuts, smallest, largest):
    def one(dim, blocks):
        heights = jax.random.uniform(jax.random.fold_in(jax.random.fold_in(stream_key, 6), dim), (blocks,), jnp.float32, smallest / len(cuts), largest / len(cuts))
        return jnp.repeat(jnp.exp(heights), dims[dim] // blocks).reshape((-1,) + (1,) * (len(dims) - dim - 1))

    gain = one(*cuts[0])
    for cut in cuts[1:]:
        gain = gain * one(*cut)
    return gain


def scatter_about(stream_key, shape, scale, limit, pieces=(), kind=jnp.bfloat16):
    gain = steps_of(stream_key, shape, pieces, -0.22, 0.18) if pieces else 1.0
    values = jax.random.normal(stream_key, shape, jnp.float32) * scale * gain
    return jnp.minimum(jnp.maximum(values, -limit), limit).astype(kind)


def setup_inputs(seed: int = 0) -> dict:
    arg_keys = jax.random.split(jax.random.key(seed), 8)
    tokens = scatter_about(arg_keys[0], (TOKENS, D), 1.0, 6.0, ((0, 8),))
    exponents = with_ends(jax.random.randint(arg_keys[1], (TOKENS, BLOCKS), -1, 2), jax.random.fold_in(arg_keys[1], 1), -1, 1).astype(jnp.int32)
    out_grad = scatter_about(arg_keys[2], (TOKENS, D), 1.0, 6.0, ((0, 8),))
    slots = draw_slots(jax.random.fold_in(arg_keys[7], 71), 0)
    gates = jnp.clip(0.1 + 0.9 * jax.random.uniform(arg_keys[4], (E, C), jnp.float32) ** steps_of(arg_keys[4], (E, C), ((0, 8),), -0.2, 0.2), 0.1, 1.0)
    w_in = scatter_about(arg_keys[5], (E, D, H), D ** -0.5, 0.15625, ((0, 8), (2, 4)))
    w_out = scatter_about(arg_keys[6], (E, H, D), H ** -0.5, 0.09375, ((0, 8), (1, 4)))
    return {"tokens": tokens, "exponents": exponents, "out_grad": out_grad, "slots": slots, "gates": gates, "w_in": w_in, "w_out": w_out}


def contract(left, right, left_dim, right_dim):
    return lax.dot_general(left, right, (((left_dim,), (right_dim,)), ((), ())), preferred_element_type=jnp.float32)

def apply_scales(values, exponents):
    row_count = values.shape[0]
    factors = jnp.exp2(exponents.astype(jnp.float32))
    widened = values.astype(jnp.float32).reshape(row_count, BLOCKS, 128) * factors[:, :, None]
    return widened.reshape(row_count, D)

def reference(tokens, exponents, out_grad, slots, gates, w_in, w_out):
    scaled = apply_scales(tokens, exponents).astype(jnp.bfloat16)

    def one_expert(accumulated, item):
        picked_rows, gate_row, weight_in, weight_out = item
        slot_rows = scaled[picked_rows]
        slot_grads = out_grad[picked_rows]
        preact = jnp.dot(slot_rows, weight_in, preferred_element_type=jnp.float32)
        hidden_full, backward = jax.vjp(jax.nn.gelu, preact)
        hidden = hidden_full.astype(jnp.bfloat16)
        upstream = contract(slot_grads, weight_out, 1, 1)
        gate_part = lax.optimization_barrier(jnp.sum(hidden.astype(jnp.float32) * upstream, axis=1))
        dpre = backward(gate_row[:, None] * upstream)[0].astype(jnp.bfloat16)
        gated_grads = (gate_row[:, None] * slot_grads.astype(jnp.float32)).astype(jnp.bfloat16)
        out_weight_grad = contract(hidden, gated_grads, 0, 0).astype(jnp.bfloat16)
        in_weight_grad = contract(slot_rows, dpre, 0, 0).astype(jnp.bfloat16)
        slot_back = contract(dpre, weight_in, 1, 1)
        accumulated = accumulated.at[picked_rows].add(slot_back)
        return (accumulated, (in_weight_grad, out_weight_grad, gate_part))
    start = jnp.zeros((TOKENS, D), jnp.float32)
    summed, (w_in_grad, w_out_grad, gate_grad) = lax.scan(one_expert, start, (slots, gates, w_in, w_out))
    token_grad = apply_scales(summed, exponents).astype(jnp.bfloat16)
    return (token_grad, w_in_grad, w_out_grad, gate_grad)
```

```python
import functools
import math

import jax
import jax.numpy as jnp
from jax import lax
from jax.experimental import pallas as pl
from jax.experimental.pallas import tpu as pltpu
from jax.sharding import PartitionSpec as P

MESH = pl.DeviceIdType.MESH
ROOT = math.sqrt(2.0 / math.pi)
CUBIC = 0.044715


def contract(left, right, left_dim, right_dim):
    return lax.dot_general(
        left, right, (((left_dim,), (right_dim,)), ((), ())), preferred_element_type=jnp.float32
    )


def apply_scales(values, exponents):
    row_count = values.shape[0]
    block_count = exponents.shape[1]
    factors = jnp.exp2(exponents.astype(jnp.float32))
    widened = values.astype(jnp.float32).reshape(row_count, block_count, 128) * factors[:, :, None]
    return widened.reshape(row_count, block_count * 128)


def local(tokens, exponents, out_grad, slots, gates, w_in, w_out):
    expert_count = lax.axis_size("expert")
    my_expert = lax.axis_index("expert")
    my_tensor = lax.axis_index("tensor")
    tok_count = tokens.shape[0]
    model_width = tokens.shape[1]
    slot_count = slots.shape[1]
    capacity = slot_count // expert_count + slot_count // (4 * expert_count)
    total_slots = expert_count * capacity
    owner = slots // tok_count
    local_index = slots % tok_count
    from_here = owner == my_expert
    send_order = jnp.cumsum(from_here.astype(jnp.int32), axis=1) - 1
    rank_range = jnp.arange(capacity, dtype=jnp.int32)
    send_hit = from_here[:, :, None] & (send_order[:, :, None] == rank_range[None, None, :])
    send_valid = jnp.any(send_hit, axis=1)
    picked_index = jnp.sum(jnp.where(send_hit, local_index[:, :, None], 0), axis=1)
    send_table = jnp.where(send_valid, picked_index, tok_count)
    row_owner = lax.dynamic_index_in_dim(owner, my_expert, 0, keepdims=False)
    slot_range = jnp.arange(slot_count, dtype=jnp.int32)
    earlier = (row_owner[:, None] == row_owner[None, :]) & (
        slot_range[:, None] > slot_range[None, :]
    )
    row_rank = jnp.sum(earlier.astype(jnp.int32), axis=1)
    flat_index = row_owner * capacity + row_rank
    scaled_local = apply_scales(tokens, exponents).astype(jnp.bfloat16)
    sent_rows = jnp.take(scaled_local, send_table, axis=0, mode="fill", fill_value=0)
    sent_grads = jnp.take(out_grad, send_table, axis=0, mode="fill", fill_value=0)
    arrived_rows, arrived_grads = (
        lax.all_to_all(sent_rows, "expert", split_axis=0, concat_axis=0, tiled=True),
        lax.all_to_all(sent_grads, "expert", split_axis=0, concat_axis=0, tiled=True),
    )
    slot_rows = arrived_rows.reshape(total_slots, model_width)
    slot_grads = arrived_grads.reshape(total_slots, model_width)
    gate_row = jnp.zeros((total_slots,), jnp.float32).at[flat_index].set(gates[0])
    weight_in = w_in[0]
    weight_out = w_out[0]
    preact = jnp.dot(slot_rows, weight_in, preferred_element_type=jnp.float32)
    hidden_full, backward = jax.vjp(jax.nn.gelu, preact)
    hidden = hidden_full.astype(jnp.bfloat16)
    upstream = contract(slot_grads, weight_out, 1, 1)
    gate_part = jnp.sum(hidden.astype(jnp.float32) * upstream, axis=1)
    gate_total = lax.psum(gate_part[flat_index], "tensor")
    dpre = backward(gate_row[:, None] * upstream)[0].astype(jnp.bfloat16)
    gated_grads = (gate_row[:, None] * slot_grads.astype(jnp.float32)).astype(jnp.bfloat16)
    out_weight_grad = contract(hidden, gated_grads, 0, 0).astype(jnp.bfloat16)
    in_weight_grad = contract(slot_rows, dpre, 0, 0).astype(jnp.bfloat16)
    slot_back = contract(dpre, weight_in, 1, 1)
    flat_send = send_table.reshape(-1)
    came_back = lax.all_to_all(
        slot_back.reshape(expert_count, capacity, model_width),
        "expert",
        split_axis=0,
        concat_axis=0,
        tiled=True,
    )
    token_sums = (
        jnp.zeros((tok_count, model_width), jnp.float32)
        .at[flat_send]
        .add(came_back.reshape(total_slots, model_width), mode="drop")
    )
    my_share = lax.psum_scatter(token_sums, "tensor", scatter_dimension=0, tiled=True)
    share_rows = my_share.shape[0]
    my_scales = lax.dynamic_slice_in_dim(exponents, my_tensor * share_rows, share_rows, 0)
    token_grad = apply_scales(my_share, my_scales).astype(jnp.bfloat16)
    return (token_grad, in_weight_grad[None], out_weight_grad[None], gate_total[None])


def message(picks, extra_picks, rows):
    third = rows.shape[1] // 3
    lead = jnp.dot(picks, rows, preferred_element_type=jnp.float32)
    rest = sum(
        jnp.dot(extra_picks[c], rows[:, c * third : (c + 1) * third], preferred_element_type=jnp.float32)
        for c in range(3)
    )
    return jnp.concatenate([lead, rest], axis=1).astype(jnp.bfloat16)


def exchange_kernel(
    experts, tensors,
    tokens, exponents, out_grad, slots, gates, w_in_hbm, w_out_hbm,
    token_out, gate_out, rows_out, gated_out, hidden_out, dpre_out,
    w_in, w_out, scaled, picks, extra_picks, place, outgoing, parts, rows, preact, hidden, dpre, gated,
    core_out, core_in, side_out, side_in, back_out, back_in, last_out, last_in, gate_parts,
    load_sem, send_sem, recv_sem, pass_send, pass_recv, ret_send, ret_recv,
    back_send, back_recv, last_send, last_recv, gate_send, gate_recv, store_sem,
):
    me = lax.axis_index("expert")
    t = lax.axis_index("tensor")
    y, core = t // 2, t % 2
    buddy = 2 * y + (1 - core)
    across = 2 * (1 - y) + core
    diagonal = 2 * (1 - y) + (1 - core)
    tok_count, width = tokens.shape
    quarter = width // tensors
    third = quarter // 3
    capacity = slots.shape[1]
    lead_rows = experts * 16

    loads = [
        pltpu.make_async_copy(w_in_hbm, w_in, load_sem.at[0]),
        pltpu.make_async_copy(w_out_hbm, w_out, load_sem.at[1]),
    ]
    for load in loads:
        load.start()

    barrier = pltpu.get_barrier_semaphore()
    peers = [lax.rem(me + off, experts) for off in range(1, experts)]
    mates = [buddy, across, diagonal]
    for d in peers:
        pl.semaphore_signal(barrier, inc=1, device_id=(d, t), device_id_type=MESH)
    for m in mates:
        pl.semaphore_signal(barrier, inc=1, device_id=(me, m), device_id_type=MESH)

    tri = (
        lax.broadcasted_iota(jnp.int32, (capacity, capacity), 0)
        < lax.broadcasted_iota(jnp.int32, (capacity, capacity), 1)
    ).astype(jnp.bfloat16)

    def ranks(mask):
        ones = jnp.where(mask, 1.0, 0.0)
        before = jnp.dot(ones.astype(jnp.bfloat16), tri, preferred_element_type=jnp.float32)
        return jnp.where(mask, before, -1.0)

    all_slots = slots[...]
    local_index = all_slots - me * tok_count
    rank = ranks((local_index >= 0) & (local_index < tok_count))
    local_number = local_index.astype(jnp.float32) + 1.0
    row_id = lax.broadcasted_iota(jnp.int32, (16, capacity), 0)
    lead_target = row_id.astype(jnp.float32)
    rest_target = (16 + row_id % 4).astype(jnp.float32)
    token_id = lax.broadcasted_iota(jnp.int32, (16, tok_count), 1).astype(jnp.float32) + 1.0
    part_id = lax.broadcasted_iota(jnp.int32, (16, tok_count), 0) // 4
    for d in range(experts):
        row_rank, row_number = rank[d : d + 1, :], local_number[d : d + 1, :]
        lead = jnp.sum(jnp.where(row_rank == lead_target, row_number, 0.0), axis=1, keepdims=True)
        rest = jnp.sum(jnp.where(row_rank == rest_target, row_number, 0.0), axis=1, keepdims=True)
        span = pl.ds(d * 16, 16)
        picks[span, :] = jnp.where(lead == token_id, 1.0, 0.0).astype(jnp.bfloat16)
        rest_hit = jnp.where(rest == token_id, 1.0, 0.0)
        for c in range(3):
            extra_picks[c, span, :] = jnp.where(part_id == c, rest_hit, 0.0).astype(jnp.bfloat16)

    factors = jnp.exp2(exponents[...].astype(jnp.float32))
    for b in range(width // 128):
        cols = pl.ds(b * 128, 128)
        scaled[:, cols] = (tokens[:, cols].astype(jnp.float32) * factors[:, b : b + 1]).astype(jnp.bfloat16)

    my_cols = pl.ds(pl.multiple_of(t * quarter, 128), quarter)
    for a, source in enumerate((scaled, out_grad)):
        filled = message(picks[...], extra_picks[...], source[:, my_cols])
        outgoing[a] = filled.reshape(experts, 16, 4 * third)
    for a in range(2):
        parts[a, t, me] = outgoing[a, me]

    def send(a, d):
        return pltpu.make_async_remote_copy(
            src_ref=outgoing.at[a, d], dst_ref=parts.at[a, t, me],
            send_sem=send_sem.at[a, d], recv_sem=recv_sem.at[a, me],
            device_id=(d, t), device_id_type=MESH,
        )

    def arrival(a, k):
        return pltpu.make_async_remote_copy(
            src_ref=outgoing.at[a, k], dst_ref=parts.at[a, t, k],
            send_sem=send_sem.at[a, k], recv_sem=recv_sem.at[a, k],
            device_id=(k, t), device_id_type=MESH,
        )

    groups = experts // 2
    own_group = me // 2

    def passing(a, kind, g):
        which, mate = ((t, buddy), (t, across), (across, buddy))[kind]
        block = parts.at[a, which, pl.ds(2 * g, 2)]
        return pltpu.make_async_remote_copy(
            src_ref=block, dst_ref=block,
            send_sem=pass_send.at[a, kind, g], recv_sem=pass_recv.at[a, kind, g],
            device_id=(me, mate), device_id_type=MESH,
        )

    def passed(a, kind, g):
        which, mate = ((buddy, buddy), (across, across), (diagonal, buddy))[kind]
        block = parts.at[a, which, pl.ds(2 * g, 2)]
        return pltpu.make_async_remote_copy(
            src_ref=block, dst_ref=block,
            send_sem=pass_send.at[a, kind, g], recv_sem=pass_recv.at[a, kind, g],
            device_id=(me, mate), device_id_type=MESH,
        )

    pl.semaphore_wait(barrier, len(peers) + len(mates))
    for a in range(2):
        for d in peers:
            send(a, d).start()

    my_slots = slots[pl.ds(me, 1), :] // tok_count
    owner_id = lax.broadcasted_iota(jnp.int32, (experts, capacity), 0)
    own_rank = ranks(jnp.broadcast_to(my_slots, (experts, capacity)) == owner_id)
    lead4 = 16.0 + lax.broadcasted_iota(jnp.int32, (4, capacity), 0).astype(jnp.float32)
    for k in range(experts):
        row_rank = own_rank[k : k + 1, :]
        place[pl.ds(k * 16, 16), :] = jnp.where(row_rank == lead_target, 1.0, 0.0)
        place[pl.ds(lead_rows + k * 4, 4), :] = jnp.where(row_rank == lead4, 1.0, 0.0)
    gate_flat = jnp.sum(place[...] * gates[...], axis=1, keepdims=True)

    rest_rows = experts * 4
    j = lax.broadcasted_iota(jnp.int32, (3 * rest_rows, lead_rows), 0)
    m = lax.broadcasted_iota(jnp.int32, (3 * rest_rows, lead_rows), 1)
    jr = j % rest_rows
    unpack = (m == (jr // 4) * 16 + 4 * (j // rest_rows) + jr % 4).astype(jnp.bfloat16)

    hidden_block = 256
    steps = w_in.shape[1] // hidden_block

    def block_of(i):
        return pl.ds(pl.multiple_of(i * hidden_block, hidden_block), hidden_block)

    def collect(a):
        order = [lax.rem(own_group + off, groups) for off in range(groups)]
        for i, g in enumerate(order):
            if i == 0:
                arrival(a, me + 1 - 2 * (me % 2)).wait_recv()
            else:
                arrival(a, 2 * g).wait_recv()
                arrival(a, 2 * g + 1).wait_recv()
            passing(a, 1, g).start()
            passing(a, 0, g).start()
        for g in order:
            passed(a, 1, g).wait_recv()
            passing(a, 2, g).start()
        for g in order:
            passed(a, 0, g).wait_recv()
        for g in order:
            passed(a, 2, g).wait_recv()
        for q in range(tensors):
            rows[a, pl.ds(0, lead_rows), pl.ds(q * quarter, quarter)] = parts[a, q, :, :, pl.ds(0, quarter)].reshape(
                lead_rows, quarter
            )
            rest = jnp.dot(
                unpack, parts[a, q, :, :, pl.ds(quarter, third)].reshape(lead_rows, third),
                preferred_element_type=jnp.float32,
            ).astype(jnp.bfloat16)
            for c in range(3):
                rows[a, pl.ds(lead_rows, rest_rows), pl.ds(q * quarter + c * third, third)] = rest[
                    c * rest_rows : (c + 1) * rest_rows
                ]

    collect(0)
    loads[0].wait()

    def forward(i, carry):
        cols = block_of(i)
        preact[:, cols] = jnp.dot(rows[0], w_in[:, cols], preferred_element_type=jnp.float32)
        return carry

    lax.fori_loop(0, steps, forward, 0)
    collect(1)
    loads[1].wait()

    def backward(i, total):
        cols = block_of(i)
        v = preact[:, cols]
        upstream = contract(rows[1], w_out[cols, :], 1, 1)
        square = v * v
        tanh = jnp.tanh(ROOT * (v + CUBIC * v * square))
        half = 0.5 * (1.0 + tanh)
        act = (v * half).astype(jnp.bfloat16)
        slope = half + 0.5 * v * (1.0 - tanh * tanh) * (ROOT * (1.0 + 3.0 * CUBIC * square))
        hidden[:, cols] = act
        dpre[:, cols] = (gate_flat * upstream * slope).astype(jnp.bfloat16)
        return total + jnp.sum(act.astype(jnp.float32) * upstream, axis=1, keepdims=True)

    gate_part = lax.fori_loop(0, steps, backward, jnp.zeros((place.shape[0], 1), jnp.float32))

    def slot_back(q):
        return contract(dpre[...], w_in[pl.ds(pl.multiple_of(q * quarter, 128), quarter), :], 1, 1)

    def to_core(i):
        return pltpu.make_async_remote_copy(
            src_ref=core_out.at[i], dst_ref=core_in.at[i], send_sem=ret_send.at[i], recv_sem=ret_recv.at[i],
            device_id=(me, buddy), device_id_type=MESH,
        )

    to_side = pltpu.make_async_remote_copy(
        src_ref=side_out, dst_ref=side_in, send_sem=ret_send.at[2], recv_sem=ret_recv.at[2],
        device_id=(me, across), device_id_type=MESH,
    )
    core_out[0] = slot_back(diagonal).astype(jnp.bfloat16)
    to_core(0).start()
    core_out[1] = slot_back(buddy).astype(jnp.bfloat16)
    to_core(1).start()
    partial = slot_back(across)
    to_core(0).wait_recv()
    side_out[...] = (partial + core_in[0].astype(jnp.float32)).astype(jnp.bfloat16)
    to_side.start()
    mine = slot_back(t)

    gate_parts[t] = jnp.broadcast_to(jnp.sum(place[...] * gate_part, axis=0, keepdims=True), (8, capacity))

    def gate_copy(i, slot):
        return pltpu.make_async_remote_copy(
            src_ref=gate_parts.at[t], dst_ref=gate_parts.at[slot], send_sem=gate_send.at[i], recv_sem=gate_recv.at[i],
            device_id=(me, mates[i]), device_id_type=MESH,
        )

    for i in range(3):
        gate_copy(i, t).start()

    gated[...] = (gate_flat * rows[1].astype(jnp.float32)).astype(jnp.bfloat16)
    stores = [
        pltpu.make_async_copy(src, dst, store_sem.at[i])
        for i, (src, dst) in enumerate(
            ((rows.at[0], rows_out), (gated, gated_out), (hidden, hidden_out), (dpre, dpre_out))
        )
    ]
    for store in stores:
        store.start()

    to_core(1).wait_recv()
    mine = mine + core_in[1].astype(jnp.float32)
    to_side.wait_recv()
    mine = (mine + side_in[...].astype(jnp.float32)).astype(jnp.bfloat16)
    tail = mine[lead_rows:]
    packed = sum(
        contract(unpack[c * rest_rows : (c + 1) * rest_rows], tail[:, c * third : (c + 1) * third], 0, 0)
        for c in range(3)
    ).astype(jnp.bfloat16)
    back_out[...] = jnp.concatenate([mine[:lead_rows], packed], axis=1).reshape(experts, 16, 4 * third)
    back_in[me] = back_out[me]

    def give_back(d, slot):
        return pltpu.make_async_remote_copy(
            src_ref=back_out.at[d], dst_ref=back_in.at[slot], send_sem=back_send.at[d], recv_sem=back_recv.at[slot],
            device_id=(d, t), device_id_type=MESH,
        )

    for d in peers:
        give_back(d, me).start()
    for d in peers:
        give_back(d, d).wait_recv()
    sums = contract(picks[...], back_in[:, :, pl.ds(0, quarter)].reshape(lead_rows, quarter), 0, 0)
    returned = back_in[:, :, pl.ds(quarter, third)].reshape(lead_rows, third)
    block_id = lax.broadcasted_iota(jnp.int32, factors.shape, 1)
    pieces = []
    for c in range(3):
        piece = sums[:, c * third : (c + 1) * third] + contract(extra_picks[c], returned, 0, 0)
        factor = jnp.sum(jnp.where(block_id == 3 * t + c, factors, 0.0), axis=1, keepdims=True)
        pieces.append((piece * factor).astype(jnp.bfloat16))
    last_out[...] = jnp.concatenate(pieces, axis=1).reshape(tensors, tok_count // tensors, quarter)
    last_in[t] = last_out[t]

    def finish(i, slot):
        return pltpu.make_async_remote_copy(
            src_ref=last_out.at[mates[i]], dst_ref=last_in.at[slot], send_sem=last_send.at[i], recv_sem=last_recv.at[i],
            device_id=(me, mates[i]), device_id_type=MESH,
        )

    for i in range(3):
        finish(i, t).start()
    for i in range(3):
        gate_copy(i, mates[i]).wait_recv()
    gate_out[...] = (gate_parts[0] + gate_parts[1] + gate_parts[2] + gate_parts[3])[0:1]
    for i in range(3):
        finish(i, mates[i]).wait_recv()
    for q in range(tensors):
        token_out[:, pl.ds(q * quarter, quarter)] = last_in[q]

    for a in range(2):
        for d in peers:
            send(a, d).wait_send()
        for kind in range(3):
            for g in range(groups):
                passing(a, kind, g).wait_send()
    for i in range(2):
        to_core(i).wait_send()
    to_side.wait_send()
    for d in peers:
        give_back(d, me).wait_send()
    for i in range(3):
        gate_copy(i, t).wait_send()
        finish(i, t).wait_send()
    for store in stores:
        store.wait()


def exchange(experts, tensors, tokens, exponents, out_grad, slots, gates, w_in, w_out):
    tok_count, width = tokens.shape
    hid = w_in.shape[1]
    quarter = width // tensors
    wide = quarter + quarter // 3
    count = experts * 20
    bf16, f32 = jnp.bfloat16, jnp.float32
    vmem = pl.BlockSpec(memory_space=pltpu.VMEM)
    hbm = pl.BlockSpec(memory_space=pl.ANY)
    dma = pltpu.SemaphoreType.DMA
    return pl.pallas_call(
        functools.partial(exchange_kernel, experts, tensors),
        out_shape=(
            jax.ShapeDtypeStruct((tok_count // tensors, width), bf16),
            jax.ShapeDtypeStruct(gates.shape, f32),
            jax.ShapeDtypeStruct((count, width), bf16),
            jax.ShapeDtypeStruct((count, width), bf16),
            jax.ShapeDtypeStruct((count, hid), bf16),
            jax.ShapeDtypeStruct((count, hid), bf16),
        ),
        in_specs=[vmem] * 5 + [hbm] * 2,
        out_specs=(vmem, vmem, hbm, hbm, hbm, hbm),
        scratch_shapes=[
            pltpu.VMEM(w_in.shape, bf16),
            pltpu.VMEM(w_out.shape, bf16),
            pltpu.VMEM((tok_count, width), bf16),
            pltpu.VMEM((experts * 16, tok_count), bf16),
            pltpu.VMEM((3, experts * 16, tok_count), bf16),
            pltpu.VMEM((count, slots.shape[1]), f32),
            pltpu.VMEM((2, experts, 16, wide), bf16),
            pltpu.VMEM((2, tensors, experts, 16, wide), bf16),
            pltpu.VMEM((2, count, width), bf16),
            pltpu.VMEM((count, hid), f32),
            pltpu.VMEM((count, hid), bf16),
            pltpu.VMEM((count, hid), bf16),
            pltpu.VMEM((count, width), bf16),
            pltpu.VMEM((2, count, quarter), bf16),
            pltpu.VMEM((2, count, quarter), bf16),
            pltpu.VMEM((count, quarter), bf16),
            pltpu.VMEM((count, quarter), bf16),
            pltpu.VMEM((experts, 16, wide), bf16),
            pltpu.VMEM((experts, 16, wide), bf16),
            pltpu.VMEM((tensors, tok_count // tensors, quarter), bf16),
            pltpu.VMEM((tensors, tok_count // tensors, quarter), bf16),
            pltpu.VMEM((tensors, 8, slots.shape[1]), f32),
            dma((2,)),
            dma((2, experts)),
            dma((2, experts)),
            dma((2, 3, experts // 2)),
            dma((2, 3, experts // 2)),
            dma((3,)),
            dma((3,)),
            dma((experts,)),
            dma((experts,)),
            dma((3,)),
            dma((3,)),
            dma((3,)),
            dma((3,)),
            dma((4,)),
        ],
        compiler_params=pltpu.CompilerParams(
            collective_id=0, has_side_effects=True, vmem_limit_bytes=48 * 2**20
        ),
    )(tokens, exponents, out_grad, slots, gates, w_in, w_out)


def local_fused(tokens, exponents, out_grad, slots, gates, w_in, w_out):
    token_grad, gate_grad, rows, gated, hidden, dpre = exchange(
        lax.axis_size("expert"), lax.axis_size("tensor"),
        tokens, exponents, out_grad, slots, gates, w_in[0], w_out[0],
    )
    out_weight_grad = contract(hidden, gated, 0, 0).astype(jnp.bfloat16)
    in_weight_grad = contract(rows, dpre, 0, 0).astype(jnp.bfloat16)
    return (token_grad, in_weight_grad[None], out_weight_grad[None], gate_grad)


def fits_exchange(mesh):
    return mesh.shape["expert"] == 8 and mesh.shape["tensor"] == 4


def solution(mesh):
    placed = (
        P("expert", None),
        P("expert", None),
        P("expert", None),
        P(),
        P("expert", None),
        P("expert", None, "tensor"),
        P("expert", "tensor", None),
    )
    return jax.shard_map(
        local_fused if fits_exchange(mesh) else local,
        mesh=mesh,
        in_specs=placed,
        out_specs=(
            P(("expert", "tensor"), None),
            P("expert", None, "tensor"),
            P("expert", "tensor", None),
            P("expert", None),
        ),
        check_vma=False,
    )
```

```python
import functools
import math

import jax
import jax.numpy as jnp
from jax import lax
from jax.experimental import pallas as pl
from jax.experimental.pallas import tpu as pltpu
from jax.sharding import PartitionSpec as P

MESH = pl.DeviceIdType.MESH
ROOT = math.sqrt(2.0 / math.pi)
CUBIC = 0.044715


def contract(left, right, left_dim, right_dim):
    return lax.dot_general(
        left, right, (((left_dim,), (right_dim,)), ((), ())), preferred_element_type=jnp.float32
    )


def apply_scales(values, exponents):
    row_count = values.shape[0]
    block_count = exponents.shape[1]
    factors = jnp.exp2(exponents.astype(jnp.float32))
    widened = values.astype(jnp.float32).reshape(row_count, block_count, 128) * factors[:, :, None]
    return widened.reshape(row_count, block_count * 128)


def local(tokens, exponents, out_grad, slots, gates, w_in, w_out):
    expert_count = lax.axis_size("expert")
    my_expert = lax.axis_index("expert")
    my_tensor = lax.axis_index("tensor")
    tok_count = tokens.shape[0]
    model_width = tokens.shape[1]
    slot_count = slots.shape[1]
    capacity = slot_count // expert_count + slot_count // (4 * expert_count)
    total_slots = expert_count * capacity
    owner = slots // tok_count
    local_index = slots % tok_count
    from_here = owner == my_expert
    send_order = jnp.cumsum(from_here.astype(jnp.int32), axis=1) - 1
    rank_range = jnp.arange(capacity, dtype=jnp.int32)
    send_hit = from_here[:, :, None] & (send_order[:, :, None] == rank_range[None, None, :])
    send_valid = jnp.any(send_hit, axis=1)
    picked_index = jnp.sum(jnp.where(send_hit, local_index[:, :, None], 0), axis=1)
    send_table = jnp.where(send_valid, picked_index, tok_count)
    row_owner = lax.dynamic_index_in_dim(owner, my_expert, 0, keepdims=False)
    slot_range = jnp.arange(slot_count, dtype=jnp.int32)
    earlier = (row_owner[:, None] == row_owner[None, :]) & (
        slot_range[:, None] > slot_range[None, :]
    )
    row_rank = jnp.sum(earlier.astype(jnp.int32), axis=1)
    flat_index = row_owner * capacity + row_rank
    scaled_local = apply_scales(tokens, exponents).astype(jnp.bfloat16)
    sent_rows = jnp.take(scaled_local, send_table, axis=0, mode="fill", fill_value=0)
    sent_grads = jnp.take(out_grad, send_table, axis=0, mode="fill", fill_value=0)
    arrived_rows, arrived_grads = (
        lax.all_to_all(sent_rows, "expert", split_axis=0, concat_axis=0, tiled=True),
        lax.all_to_all(sent_grads, "expert", split_axis=0, concat_axis=0, tiled=True),
    )
    slot_rows = arrived_rows.reshape(total_slots, model_width)
    slot_grads = arrived_grads.reshape(total_slots, model_width)
    gate_row = jnp.zeros((total_slots,), jnp.float32).at[flat_index].set(gates[0])
    weight_in = w_in[0]
    weight_out = w_out[0]
    preact = jnp.dot(slot_rows, weight_in, preferred_element_type=jnp.float32)
    hidden_full, backward = jax.vjp(jax.nn.gelu, preact)
    hidden = hidden_full.astype(jnp.bfloat16)
    upstream = contract(slot_grads, weight_out, 1, 1)
    gate_part = jnp.sum(hidden.astype(jnp.float32) * upstream, axis=1)
    gate_total = lax.psum(gate_part[flat_index], "tensor")
    dpre = backward(gate_row[:, None] * upstream)[0].astype(jnp.bfloat16)
    gated_grads = (gate_row[:, None] * slot_grads.astype(jnp.float32)).astype(jnp.bfloat16)
    out_weight_grad = contract(hidden, gated_grads, 0, 0).astype(jnp.bfloat16)
    in_weight_grad = contract(slot_rows, dpre, 0, 0).astype(jnp.bfloat16)
    slot_back = contract(dpre, weight_in, 1, 1)
    flat_send = send_table.reshape(-1)
    came_back = lax.all_to_all(
        slot_back.reshape(expert_count, capacity, model_width),
        "expert",
        split_axis=0,
        concat_axis=0,
        tiled=True,
    )
    token_sums = (
        jnp.zeros((tok_count, model_width), jnp.float32)
        .at[flat_send]
        .add(came_back.reshape(total_slots, model_width), mode="drop")
    )
    my_share = lax.psum_scatter(token_sums, "tensor", scatter_dimension=0, tiled=True)
    share_rows = my_share.shape[0]
    my_scales = lax.dynamic_slice_in_dim(exponents, my_tensor * share_rows, share_rows, 0)
    token_grad = apply_scales(my_share, my_scales).astype(jnp.bfloat16)
    return (token_grad, in_weight_grad[None], out_weight_grad[None], gate_total[None])


def message(picks, extra_picks, rows):
    third = rows.shape[1] // 3
    lead = jnp.dot(picks, rows, preferred_element_type=jnp.float32)
    rest = sum(
        jnp.dot(extra_picks[c], rows[:, c * third : (c + 1) * third], preferred_element_type=jnp.float32)
        for c in range(3)
    )
    return jnp.concatenate([lead, rest], axis=1).astype(jnp.bfloat16)


def exchange_kernel(
    experts, tensors,
    tokens_hbm, exponents_hbm, out_grad_hbm, slots_hbm, gates_hbm, w_in_hbm, w_out_hbm,
    token_out, gate_out, rows_out, gated_out, hidden_out, dpre_out,
    token_held, gate_held, rows, gated, hidden, dpre,
    tokens, exponents, out_grad, slots, gates,
    w_in, w_out, scaled, picks, extra_picks, place, outgoing, parts, grads, preact,
    core_out, core_in, side_out, side_in, mine, back_out, back_in, last_out, last_in, gate_parts,
    load_sem, send_sem, recv_sem, pass_send, pass_recv, ret_send, ret_recv, side_send, side_recv,
    back_send, back_recv, last_send, last_recv, gate_send, gate_recv, store_sem,
):
    me = lax.axis_index("expert")
    t = lax.axis_index("tensor")
    y, core = t // 2, t % 2
    buddy = 2 * y + (1 - core)
    across = 2 * (1 - y) + core
    diagonal = 2 * (1 - y) + (1 - core)
    tok_count, width = tokens.shape
    quarter = width // tensors
    third = quarter // 3
    capacity = slots.shape[1]
    lead_rows = experts * 16

    loads = [
        pltpu.make_async_copy(source, held, load_sem.at[i])
        for i, (source, held) in enumerate(
            (
                (slots_hbm, slots), (exponents_hbm, exponents), (tokens_hbm, tokens), (out_grad_hbm, out_grad),
                (gates_hbm, gates), (w_in_hbm, w_in), (w_out_hbm, w_out),
            )
        )
    ]
    for load in loads:
        load.start()

    barrier = pltpu.get_barrier_semaphore()
    z, x = me // 2, me % 2
    order = [(z + 2) % 4, 3 - z, z + 1 - 2 * (z % 2), z]
    partner = 2 * z + 1 - x
    peers = [2 * g + i for g in order[:3] for i in (x, 1 - x)] + [partner]
    mates = [buddy, across, diagonal]
    for d in peers:
        pl.semaphore_signal(barrier, inc=1, device_id=(d, t), device_id_type=MESH)
    for m in mates:
        pl.semaphore_signal(barrier, inc=1, device_id=(me, m), device_id_type=MESH)

    tri = (
        lax.broadcasted_iota(jnp.int32, (capacity, capacity), 0)
        < lax.broadcasted_iota(jnp.int32, (capacity, capacity), 1)
    ).astype(jnp.bfloat16)

    def ranks(mask):
        ones = jnp.where(mask, 1.0, 0.0)
        before = jnp.dot(ones.astype(jnp.bfloat16), tri, preferred_element_type=jnp.float32)
        return jnp.where(mask, before, -1.0)

    loads[0].wait()
    all_slots = slots[...]
    local_index = all_slots - me * tok_count
    rank = ranks((local_index >= 0) & (local_index < tok_count))
    local_number = local_index.astype(jnp.float32) + 1.0
    row_id = lax.broadcasted_iota(jnp.int32, (16, capacity), 0)
    lead_target = row_id.astype(jnp.float32)
    rest_target = (16 + row_id % 4).astype(jnp.float32)
    token_id = lax.broadcasted_iota(jnp.int32, (16, tok_count), 1).astype(jnp.float32) + 1.0
    part_id = lax.broadcasted_iota(jnp.int32, (16, tok_count), 0) // 4
    for d in range(experts):
        row_rank, row_number = rank[d : d + 1, :], local_number[d : d + 1, :]
        lead = jnp.sum(jnp.where(row_rank == lead_target, row_number, 0.0), axis=1, keepdims=True)
        rest = jnp.sum(jnp.where(row_rank == rest_target, row_number, 0.0), axis=1, keepdims=True)
        span = pl.ds(d * 16, 16)
        picks[span, :] = jnp.where(lead == token_id, 1.0, 0.0).astype(jnp.bfloat16)
        rest_hit = jnp.where(rest == token_id, 1.0, 0.0)
        for c in range(3):
            extra_picks[c, span, :] = jnp.where(part_id == c, rest_hit, 0.0).astype(jnp.bfloat16)

    blocks = exponents.shape[0]
    eye = (
        lax.broadcasted_iota(jnp.int32, (blocks, blocks), 0) == lax.broadcasted_iota(jnp.int32, (blocks, blocks), 1)
    ).astype(jnp.bfloat16)
    loads[1].wait()
    factors = contract(jnp.exp2(exponents[...].astype(jnp.float32)).astype(jnp.bfloat16), eye, 0, 0)
    loads[2].wait()
    for b in range(width // 128):
        cols = pl.ds(b * 128, 128)
        scaled[:, cols] = (tokens[:, cols].astype(jnp.float32) * factors[:, b : b + 1]).astype(jnp.bfloat16)

    loads[3].wait()
    my_cols = pl.ds(pl.multiple_of(t * quarter, 128), quarter)
    for a, source in enumerate((scaled, out_grad)):
        filled = message(picks[...], extra_picks[...], source[:, my_cols])
        outgoing[a] = filled.reshape(experts, 16, 4 * third)
    for a in range(2):
        parts[a, t, me] = outgoing[a, me]

    def send(a, d):
        return pltpu.make_async_remote_copy(
            src_ref=outgoing.at[a, d], dst_ref=parts.at[a, t, me],
            send_sem=send_sem.at[a, d], recv_sem=recv_sem.at[a, me],
            device_id=(d, t), device_id_type=MESH,
        )

    def arrival(a, k):
        return pltpu.make_async_remote_copy(
            src_ref=outgoing.at[a, k], dst_ref=parts.at[a, t, k],
            send_sem=send_sem.at[a, k], recv_sem=recv_sem.at[a, k],
            device_id=(k, t), device_id_type=MESH,
        )

    groups = experts // 2

    def passing(a, kind, g):
        which, mate = ((t, buddy), (t, across), (across, buddy))[kind]
        block = parts.at[a, which, pl.ds(2 * g, 2)]
        return pltpu.make_async_remote_copy(
            src_ref=block, dst_ref=block,
            send_sem=pass_send.at[a, kind, g], recv_sem=pass_recv.at[a, kind, g],
            device_id=(me, mate), device_id_type=MESH,
        )

    def passed(a, kind, g):
        which, mate = ((buddy, buddy), (across, across), (diagonal, buddy))[kind]
        block = parts.at[a, which, pl.ds(2 * g, 2)]
        return pltpu.make_async_remote_copy(
            src_ref=block, dst_ref=block,
            send_sem=pass_send.at[a, kind, g], recv_sem=pass_recv.at[a, kind, g],
            device_id=(me, mate), device_id_type=MESH,
        )

    pl.semaphore_wait(barrier, len(peers) + len(mates))
    for a in range(2):
        for d in peers:
            send(a, d).start()

    my_slots = slots[pl.ds(me, 1), :] // tok_count
    owner_id = lax.broadcasted_iota(jnp.int32, (experts, capacity), 0)
    own_rank = ranks(jnp.broadcast_to(my_slots, (experts, capacity)) == owner_id)
    lead4 = 16.0 + lax.broadcasted_iota(jnp.int32, (4, capacity), 0).astype(jnp.float32)
    for k in range(experts):
        row_rank = own_rank[k : k + 1, :]
        place[pl.ds(k * 16, 16), :] = jnp.where(row_rank == lead_target, 1.0, 0.0)
        place[pl.ds(lead_rows + k * 4, 4), :] = jnp.where(row_rank == lead4, 1.0, 0.0)
    loads[4].wait()
    gate_flat = jnp.sum(place[...] * gates[...], axis=1, keepdims=True)

    rest_rows = experts * 4
    j = lax.broadcasted_iota(jnp.int32, (3 * rest_rows, lead_rows), 0)
    m = lax.broadcasted_iota(jnp.int32, (3 * rest_rows, lead_rows), 1)
    jr = j % rest_rows
    unpack = (m == (jr // 4) * 16 + 4 * (j // rest_rows) + jr % 4).astype(jnp.bfloat16)

    hidden_block = w_in.shape[1] // groups

    def block_of(i):
        return pl.ds(pl.multiple_of(i * hidden_block, hidden_block), hidden_block)

    near_first = [order[3], order[2], order[0], order[1]]
    for a in range(2):
        for i, g in enumerate(near_first):
            if i == 0:
                arrival(a, partner).wait_recv()
            else:
                arrival(a, 2 * g).wait_recv()
                arrival(a, 2 * g + 1).wait_recv()
            passing(a, 1, g).start()
            passing(a, 0, g).start()

    def relay(a, g):
        passed(a, 1, g).wait_recv()
        passing(a, 2, g).start()

    def arrange(a, target):
        for g in near_first:
            passed(a, 0, g).wait_recv()
        for g in near_first:
            passed(a, 2, g).wait_recv()
        for q in range(tensors):
            target[pl.ds(0, lead_rows), pl.ds(q * quarter, quarter)] = parts[a, q, :, :, pl.ds(0, quarter)].reshape(
                lead_rows, quarter
            )
            rest = jnp.dot(
                unpack, parts[a, q, :, :, pl.ds(quarter, third)].reshape(lead_rows, third),
                preferred_element_type=jnp.float32,
            ).astype(jnp.bfloat16)
            for c in range(3):
                target[pl.ds(lead_rows, rest_rows), pl.ds(q * quarter + c * third, third)] = rest[
                    c * rest_rows : (c + 1) * rest_rows
                ]

    for g in near_first:
        relay(0, g)
    arrange(0, rows)
    loads[5].wait()
    for i, g in enumerate(near_first):
        cols = pl.ds(i * hidden_block, hidden_block)
        preact[:, cols] = jnp.dot(rows[...], w_in[:, cols], preferred_element_type=jnp.float32)
        relay(1, g)
    arrange(1, grads)
    loads[6].wait()

    def backward(i, total):
        cols = block_of(i)
        v = preact[:, cols]
        upstream = contract(grads[...], w_out[cols, :], 1, 1)
        square = v * v
        tanh = jnp.tanh(ROOT * (v + CUBIC * v * square))
        half = 0.5 * (1.0 + tanh)
        act = (v * half).astype(jnp.bfloat16)
        slope = half + 0.5 * v * (1.0 - tanh * tanh) * (ROOT * (1.0 + 3.0 * CUBIC * square))
        hidden[:, cols] = act
        dpre[:, cols] = (gate_flat * upstream * slope).astype(jnp.bfloat16)
        return total + jnp.sum(act.astype(jnp.float32) * upstream, axis=1, keepdims=True)

    gate_part = lax.fori_loop(0, groups, backward, jnp.zeros((place.shape[0], 1), jnp.float32))

    def slot_back(q):
        return contract(dpre[...], w_in[pl.ds(pl.multiple_of(q * quarter, 128), quarter), :], 1, 1)

    def to_core(i):
        return pltpu.make_async_remote_copy(
            src_ref=core_out.at[i], dst_ref=core_in.at[i], send_sem=ret_send.at[i], recv_sem=ret_recv.at[i],
            device_id=(me, buddy), device_id_type=MESH,
        )

    spans = [pl.ds(lead_rows, rest_rows)] + [pl.ds(pl.multiple_of(32 * g, 32), 32) for g in order]

    def to_side(i):
        return pltpu.make_async_remote_copy(
            src_ref=side_out.at[spans[i]], dst_ref=side_in.at[spans[i]],
            send_sem=side_send.at[i], recv_sem=side_recv.at[i],
            device_id=(me, across), device_id_type=MESH,
        )

    core_out[0] = slot_back(diagonal).astype(jnp.bfloat16)
    to_core(0).start()
    partial = slot_back(across)
    to_core(0).wait_recv()
    side_out[...] = (partial + core_in[0].astype(jnp.float32)).astype(jnp.bfloat16)
    for i in range(len(spans)):
        to_side(i).start()
    core_out[1] = slot_back(buddy).astype(jnp.bfloat16)
    to_core(1).start()
    mine[...] = slot_back(t)

    gate_parts[t] = jnp.broadcast_to(jnp.sum(place[...] * gate_part, axis=0, keepdims=True), (8, capacity))

    def gate_copy(i, slot):
        return pltpu.make_async_remote_copy(
            src_ref=gate_parts.at[t], dst_ref=gate_parts.at[slot], send_sem=gate_send.at[i], recv_sem=gate_recv.at[i],
            device_id=(me, mates[i]), device_id_type=MESH,
        )

    for i in range(3):
        gate_copy(i, t).start()

    def store(i):
        held, out = (
            (rows, rows_out), (dpre, dpre_out), (hidden, hidden_out), (gated, gated_out),
            (gate_held, gate_out), (token_held, token_out),
        )[i]
        return pltpu.make_async_copy(held, out, store_sem.at[i])

    gated[...] = (gate_flat * grads[...].astype(jnp.float32)).astype(jnp.bfloat16)
    for i in range(4):
        store(i).start()
    to_core(1).wait_recv()
    mine[...] += core_in[1].astype(jnp.float32)

    def total(i):
        to_side(i).wait_recv()
        return (mine[spans[i], :] + side_in[spans[i], :].astype(jnp.float32)).astype(jnp.bfloat16)

    def give_back(d, slot):
        return pltpu.make_async_remote_copy(
            src_ref=back_out.at[d], dst_ref=back_in.at[slot], send_sem=back_send.at[d], recv_sem=back_recv.at[slot],
            device_id=(d, t), device_id_type=MESH,
        )

    tail = total(0)
    packed = sum(
        contract(unpack[c * rest_rows : (c + 1) * rest_rows], tail[:, c * third : (c + 1) * third], 0, 0)
        for c in range(3)
    ).astype(jnp.bfloat16)
    back_out[:, :, pl.ds(quarter, third)] = packed.reshape(experts, 16, third)
    for i, g in enumerate(order):
        back_out[pl.ds(2 * g, 2), :, pl.ds(0, quarter)] = total(i + 1).reshape(2, 16, quarter)
        if i < 3:
            give_back(2 * g, me).start()
            give_back(2 * g + 1, me).start()
        else:
            give_back(partner, me).start()
            back_in[me] = back_out[me]
    for d in peers:
        give_back(d, d).wait_recv()
    sums = contract(picks[...], back_in[:, :, pl.ds(0, quarter)].reshape(lead_rows, quarter), 0, 0)
    returned = back_in[:, :, pl.ds(quarter, third)].reshape(lead_rows, third)
    block_id = lax.broadcasted_iota(jnp.int32, factors.shape, 1)
    pieces = []
    for c in range(3):
        piece = sums[:, c * third : (c + 1) * third] + contract(extra_picks[c], returned, 0, 0)
        factor = jnp.sum(jnp.where(block_id == 3 * t + c, factors, 0.0), axis=1, keepdims=True)
        pieces.append((piece * factor).astype(jnp.bfloat16))
    last_out[...] = jnp.concatenate(pieces, axis=1).reshape(tensors, tok_count // tensors, quarter)
    last_in[t] = last_out[t]

    def finish(i, slot):
        return pltpu.make_async_remote_copy(
            src_ref=last_out.at[mates[i]], dst_ref=last_in.at[slot], send_sem=last_send.at[i], recv_sem=last_recv.at[i],
            device_id=(me, mates[i]), device_id_type=MESH,
        )

    for i in range(3):
        finish(i, t).start()
    for i in range(3):
        gate_copy(i, mates[i]).wait_recv()
    gate_held[...] = (gate_parts[0] + gate_parts[1] + gate_parts[2] + gate_parts[3])[0:1]
    store(4).start()
    for i in range(3):
        finish(i, mates[i]).wait_recv()
    for q in range(tensors):
        token_held[:, pl.ds(q * quarter, quarter)] = last_in[q]
    store(5).start()

    for a in range(2):
        for d in peers:
            send(a, d).wait_send()
        for kind in range(3):
            for g in range(groups):
                passing(a, kind, g).wait_send()
    for i in range(2):
        to_core(i).wait_send()
    for i in range(len(spans)):
        to_side(i).wait_send()
    for d in peers:
        give_back(d, me).wait_send()
    for i in range(3):
        gate_copy(i, t).wait_send()
        finish(i, t).wait_send()
    for i in range(6):
        store(i).wait()


def exchange(experts, tensors, tokens, exponents, out_grad, slots, gates, w_in, w_out):
    tok_count, width = tokens.shape
    hid = w_in.shape[1]
    quarter = width // tensors
    wide = quarter + quarter // 3
    count = experts * 20
    bf16, f32 = jnp.bfloat16, jnp.float32
    hbm = pl.BlockSpec(memory_space=pltpu.HBM)
    dma = pltpu.SemaphoreType.DMA
    return pl.pallas_call(
        functools.partial(exchange_kernel, experts, tensors),
        out_shape=(
            jax.ShapeDtypeStruct((tok_count // tensors, width), bf16),
            jax.ShapeDtypeStruct(gates.shape, f32),
            jax.ShapeDtypeStruct((count, width), bf16),
            jax.ShapeDtypeStruct((count, width), bf16),
            jax.ShapeDtypeStruct((count, hid), bf16),
            jax.ShapeDtypeStruct((count, hid), bf16),
        ),
        in_specs=[hbm] * 7,
        out_specs=(hbm,) * 6,
        scratch_shapes=[
            pltpu.VMEM((tok_count // tensors, width), bf16),
            pltpu.VMEM(gates.shape, f32),
            pltpu.VMEM((count, width), bf16),
            pltpu.VMEM((count, width), bf16),
            pltpu.VMEM((count, hid), bf16),
            pltpu.VMEM((count, hid), bf16),
            pltpu.VMEM(tokens.shape, bf16),
            pltpu.VMEM(exponents.shape, jnp.int32),
            pltpu.VMEM(out_grad.shape, bf16),
            pltpu.VMEM(slots.shape, jnp.int32),
            pltpu.VMEM(gates.shape, f32),
            pltpu.VMEM(w_in.shape, bf16),
            pltpu.VMEM(w_out.shape, bf16),
            pltpu.VMEM((tok_count, width), bf16),
            pltpu.VMEM((experts * 16, tok_count), bf16),
            pltpu.VMEM((3, experts * 16, tok_count), bf16),
            pltpu.VMEM((count, slots.shape[1]), f32),
            pltpu.VMEM((2, experts, 16, wide), bf16),
            pltpu.VMEM((2, tensors, experts, 16, wide), bf16),
            pltpu.VMEM((count, width), bf16),
            pltpu.VMEM((count, hid), f32),
            pltpu.VMEM((2, count, quarter), bf16),
            pltpu.VMEM((2, count, quarter), bf16),
            pltpu.VMEM((count, quarter), bf16),
            pltpu.VMEM((count, quarter), bf16),
            pltpu.VMEM((count, quarter), f32),
            pltpu.VMEM((experts, 16, wide), bf16),
            pltpu.VMEM((experts, 16, wide), bf16),
            pltpu.VMEM((tensors, tok_count // tensors, quarter), bf16),
            pltpu.VMEM((tensors, tok_count // tensors, quarter), bf16),
            pltpu.VMEM((tensors, 8, slots.shape[1]), f32),
            dma((7,)),
            dma((2, experts)),
            dma((2, experts)),
            dma((2, 3, experts // 2)),
            dma((2, 3, experts // 2)),
            dma((2,)),
            dma((2,)),
            dma((5,)),
            dma((5,)),
            dma((experts,)),
            dma((experts,)),
            dma((3,)),
            dma((3,)),
            dma((3,)),
            dma((3,)),
            dma((6,)),
        ],
        compiler_params=pltpu.CompilerParams(
            collective_id=0, has_side_effects=True, vmem_limit_bytes=60 * 2**20
        ),
    )(tokens, exponents, out_grad, slots, gates, w_in, w_out)


def weights_kernel(
    token_hbm, gate_hbm, rows_hbm, gated_hbm, hidden_hbm, dpre_hbm,
    token_out, gate_out, in_out, out_out,
    rows, gated, hidden, dpre, token_held, gate_held, in_held, out_held, load_sem, sem,
):
    sources = (hidden_hbm, gated_hbm, rows_hbm, dpre_hbm, token_hbm, gate_hbm)
    helds = (hidden, gated, rows, dpre, token_held, gate_held)
    loads = [
        pltpu.make_async_copy(source, held, load_sem.at[i]) for i, (source, held) in enumerate(zip(sources, helds))
    ]
    for load in loads:
        load.start()
    chunks = 4
    copies = []
    for n, (left, right, held, out) in enumerate(((hidden, gated, out_held, out_out), (rows, dpre, in_held, in_out))):
        loads[2 * n].wait()
        loads[2 * n + 1].wait()
        for i in range(chunks):
            size = out.shape[0] // chunks
            span = pl.ds(i * size, size)
            held[span, :] = contract(left[:, span], right[...], 0, 0).astype(jnp.bfloat16)
            copies.append(pltpu.make_async_copy(held.at[span], out.at[span], sem.at[len(copies)]))
            copies[-1].start()
        if n == 0:
            for i, (held, out) in enumerate(((token_held, token_out), (gate_held, gate_out))):
                loads[4 + i].wait()
                copies.append(pltpu.make_async_copy(held, out, sem.at[len(copies)]))
                copies[-1].start()
    for copy in copies:
        copy.wait()


def weight_grads(token_grad, gate_grad, rows, gated, hidden, dpre):
    width, hid = rows.shape[1], hidden.shape[1]
    bf16 = jnp.bfloat16
    like = lambda array: jax.ShapeDtypeStruct(array.shape, array.dtype)
    hbm = pl.BlockSpec(memory_space=pltpu.HBM)
    return pl.pallas_call(
        weights_kernel,
        out_shape=(
            like(token_grad), like(gate_grad),
            jax.ShapeDtypeStruct((width, hid), bf16), jax.ShapeDtypeStruct((hid, width), bf16),
        ),
        in_specs=[hbm] * 6,
        out_specs=(hbm,) * 4,
        scratch_shapes=[
            pltpu.VMEM(array.shape, array.dtype) for array in (rows, gated, hidden, dpre, token_grad, gate_grad)
        ]
        + [
            pltpu.VMEM((width, hid), bf16),
            pltpu.VMEM((hid, width), bf16),
            pltpu.SemaphoreType.DMA((6,)),
            pltpu.SemaphoreType.DMA((10,)),
        ],
        compiler_params=pltpu.CompilerParams(vmem_limit_bytes=60 * 2**20),
    )(token_grad, gate_grad, rows, gated, hidden, dpre)


def local_fused(tokens, exponents, out_grad, slots, gates, w_in, w_out):
    results = exchange(
        lax.axis_size("expert"), lax.axis_size("tensor"),
        tokens, exponents.T, out_grad, slots, gates, w_in[0], w_out[0],
    )
    token_grad, gate_grad, in_weight_grad, out_weight_grad = weight_grads(*results)
    return (token_grad, in_weight_grad[None], out_weight_grad[None], gate_grad)


def fits_exchange(mesh):
    return mesh.shape["expert"] == 8 and mesh.shape["tensor"] == 4


def solution(mesh):
    placed = (
        P("expert", None),
        P("expert", None),
        P("expert", None),
        P(),
        P("expert", None),
        P("expert", None, "tensor"),
        P("expert", "tensor", None),
    )
    return jax.shard_map(
        local_fused if fits_exchange(mesh) else local,
        mesh=mesh,
        in_specs=placed,
        out_specs=(
            P(("expert", "tensor"), None),
            P("expert", None, "tensor"),
            P("expert", "tensor", None),
            P("expert", None),
        ),
        check_vma=False,
    )
```

```python
import functools
import math

import jax
import jax.numpy as jnp
from jax import lax
from jax.experimental import pallas as pl
from jax.experimental.pallas import tpu as pltpu
from jax.sharding import PartitionSpec as P

MESH = pl.DeviceIdType.MESH
ROOT = math.sqrt(2.0 / math.pi)
CUBIC = 0.044715


def contract(left, right, left_dim, right_dim):
    return lax.dot_general(
        left, right, (((left_dim,), (right_dim,)), ((), ())), preferred_element_type=jnp.float32
    )


def apply_scales(values, exponents):
    row_count = values.shape[0]
    block_count = exponents.shape[1]
    factors = jnp.exp2(exponents.astype(jnp.float32))
    widened = values.astype(jnp.float32).reshape(row_count, block_count, 128) * factors[:, :, None]
    return widened.reshape(row_count, block_count * 128)


def local(tokens, exponents, out_grad, slots, gates, w_in, w_out):
    expert_count = lax.axis_size("expert")
    my_expert = lax.axis_index("expert")
    my_tensor = lax.axis_index("tensor")
    tok_count = tokens.shape[0]
    model_width = tokens.shape[1]
    slot_count = slots.shape[1]
    capacity = slot_count // expert_count + slot_count // (4 * expert_count)
    total_slots = expert_count * capacity
    owner = slots // tok_count
    local_index = slots % tok_count
    from_here = owner == my_expert
    send_order = jnp.cumsum(from_here.astype(jnp.int32), axis=1) - 1
    rank_range = jnp.arange(capacity, dtype=jnp.int32)
    send_hit = from_here[:, :, None] & (send_order[:, :, None] == rank_range[None, None, :])
    send_valid = jnp.any(send_hit, axis=1)
    picked_index = jnp.sum(jnp.where(send_hit, local_index[:, :, None], 0), axis=1)
    send_table = jnp.where(send_valid, picked_index, tok_count)
    row_owner = lax.dynamic_index_in_dim(owner, my_expert, 0, keepdims=False)
    slot_range = jnp.arange(slot_count, dtype=jnp.int32)
    earlier = (row_owner[:, None] == row_owner[None, :]) & (
        slot_range[:, None] > slot_range[None, :]
    )
    row_rank = jnp.sum(earlier.astype(jnp.int32), axis=1)
    flat_index = row_owner * capacity + row_rank
    scaled_local = apply_scales(tokens, exponents).astype(jnp.bfloat16)
    sent_rows = jnp.take(scaled_local, send_table, axis=0, mode="fill", fill_value=0)
    sent_grads = jnp.take(out_grad, send_table, axis=0, mode="fill", fill_value=0)
    arrived_rows, arrived_grads = (
        lax.all_to_all(sent_rows, "expert", split_axis=0, concat_axis=0, tiled=True),
        lax.all_to_all(sent_grads, "expert", split_axis=0, concat_axis=0, tiled=True),
    )
    slot_rows = arrived_rows.reshape(total_slots, model_width)
    slot_grads = arrived_grads.reshape(total_slots, model_width)
    gate_row = jnp.zeros((total_slots,), jnp.float32).at[flat_index].set(gates[0])
    weight_in = w_in[0]
    weight_out = w_out[0]
    preact = jnp.dot(slot_rows, weight_in, preferred_element_type=jnp.float32)
    hidden_full, backward = jax.vjp(jax.nn.gelu, preact)
    hidden = hidden_full.astype(jnp.bfloat16)
    upstream = contract(slot_grads, weight_out, 1, 1)
    gate_part = jnp.sum(hidden.astype(jnp.float32) * upstream, axis=1)
    gate_total = lax.psum(gate_part[flat_index], "tensor")
    dpre = backward(gate_row[:, None] * upstream)[0].astype(jnp.bfloat16)
    gated_grads = (gate_row[:, None] * slot_grads.astype(jnp.float32)).astype(jnp.bfloat16)
    out_weight_grad = contract(hidden, gated_grads, 0, 0).astype(jnp.bfloat16)
    in_weight_grad = contract(slot_rows, dpre, 0, 0).astype(jnp.bfloat16)
    slot_back = contract(dpre, weight_in, 1, 1)
    flat_send = send_table.reshape(-1)
    came_back = lax.all_to_all(
        slot_back.reshape(expert_count, capacity, model_width),
        "expert",
        split_axis=0,
        concat_axis=0,
        tiled=True,
    )
    token_sums = (
        jnp.zeros((tok_count, model_width), jnp.float32)
        .at[flat_send]
        .add(came_back.reshape(total_slots, model_width), mode="drop")
    )
    my_share = lax.psum_scatter(token_sums, "tensor", scatter_dimension=0, tiled=True)
    share_rows = my_share.shape[0]
    my_scales = lax.dynamic_slice_in_dim(exponents, my_tensor * share_rows, share_rows, 0)
    token_grad = apply_scales(my_share, my_scales).astype(jnp.bfloat16)
    return (token_grad, in_weight_grad[None], out_weight_grad[None], gate_total[None])


def message(picks, extra_picks, rows):
    third = rows.shape[1] // 3
    lead = jnp.dot(picks, rows, preferred_element_type=jnp.float32)
    rest = sum(
        jnp.dot(extra_picks[c], rows[:, c * third : (c + 1) * third], preferred_element_type=jnp.float32)
        for c in range(3)
    )
    return jnp.concatenate([lead, rest], axis=1).astype(jnp.bfloat16)


def exchange_kernel(
    experts, tensors,
    tokens_hbm, exponents_hbm, out_grad_hbm, slots_hbm, gates_hbm, w_in_hbm, w_out_hbm,
    token_out, gate_out, rows_out, dpre_out, weight_out,
    token_held, gate_held, rows, gated, hidden, dpre,
    tokens, exponents, out_grad, slots, gates,
    w_in, w_out, scaled, picks, extra_picks, place, outgoing, parts, grads, slope, upstream, weight_held,
    core_out, core_in, side_out, side_in, mine, back_out, back_in, last_out, last_in, gate_parts,
    load_sem, send_sem, recv_sem, pass_send, pass_recv, ret_send, ret_recv, side_send, side_recv,
    back_send, back_recv, last_send, last_recv, gate_send, gate_recv, store_sem,
):
    me = lax.axis_index("expert")
    t = lax.axis_index("tensor")
    y, core = t // 2, t % 2
    buddy = 2 * y + (1 - core)
    across = 2 * (1 - y) + core
    diagonal = 2 * (1 - y) + (1 - core)
    tok_count, width = tokens.shape
    quarter = width // tensors
    third = quarter // 3
    capacity = slots.shape[1]
    lead_rows = experts * 16

    loads = [
        pltpu.make_async_copy(source, held, load_sem.at[i])
        for i, (source, held) in enumerate(
            (
                (slots_hbm, slots), (exponents_hbm, exponents), (tokens_hbm, tokens), (out_grad_hbm, out_grad),
                (gates_hbm, gates), (w_in_hbm, w_in), (w_out_hbm, w_out),
            )
        )
    ]
    for load in loads:
        load.start()

    barrier = pltpu.get_barrier_semaphore()
    z, x = me // 2, me % 2
    order = [(z + 2) % 4, 3 - z, z + 1 - 2 * (z % 2), z]
    partner = 2 * z + 1 - x
    peers = [2 * g + i for g in order[:3] for i in (x, 1 - x)] + [partner]
    mates = [buddy, across, diagonal]
    for d in peers:
        pl.semaphore_signal(barrier, inc=1, device_id=(d, t), device_id_type=MESH)
    for m in mates:
        pl.semaphore_signal(barrier, inc=1, device_id=(me, m), device_id_type=MESH)

    tri = (
        lax.broadcasted_iota(jnp.int32, (capacity, capacity), 0)
        < lax.broadcasted_iota(jnp.int32, (capacity, capacity), 1)
    ).astype(jnp.bfloat16)

    def ranks(mask):
        ones = jnp.where(mask, 1.0, 0.0)
        before = jnp.dot(ones.astype(jnp.bfloat16), tri, preferred_element_type=jnp.float32)
        return jnp.where(mask, before, -1.0)

    loads[0].wait()
    all_slots = slots[...]
    local_index = all_slots - me * tok_count
    rank = ranks((local_index >= 0) & (local_index < tok_count))
    local_number = local_index.astype(jnp.float32) + 1.0
    row_id = lax.broadcasted_iota(jnp.int32, (16, capacity), 0)
    lead_target = row_id.astype(jnp.float32)
    rest_target = (16 + row_id % 4).astype(jnp.float32)
    token_id = lax.broadcasted_iota(jnp.int32, (16, tok_count), 1).astype(jnp.float32) + 1.0
    part_id = lax.broadcasted_iota(jnp.int32, (16, tok_count), 0) // 4
    for d in range(experts):
        row_rank, row_number = rank[d : d + 1, :], local_number[d : d + 1, :]
        lead = jnp.sum(jnp.where(row_rank == lead_target, row_number, 0.0), axis=1, keepdims=True)
        rest = jnp.sum(jnp.where(row_rank == rest_target, row_number, 0.0), axis=1, keepdims=True)
        span = pl.ds(d * 16, 16)
        picks[span, :] = jnp.where(lead == token_id, 1.0, 0.0).astype(jnp.bfloat16)
        rest_hit = jnp.where(rest == token_id, 1.0, 0.0)
        for c in range(3):
            extra_picks[c, span, :] = jnp.where(part_id == c, rest_hit, 0.0).astype(jnp.bfloat16)

    blocks = exponents.shape[0]
    eye = (
        lax.broadcasted_iota(jnp.int32, (blocks, blocks), 0) == lax.broadcasted_iota(jnp.int32, (blocks, blocks), 1)
    ).astype(jnp.bfloat16)
    loads[1].wait()
    factors = contract(jnp.exp2(exponents[...].astype(jnp.float32)).astype(jnp.bfloat16), eye, 0, 0)
    loads[2].wait()
    for b in range(width // 128):
        cols = pl.ds(b * 128, 128)
        scaled[:, cols] = (tokens[:, cols].astype(jnp.float32) * factors[:, b : b + 1]).astype(jnp.bfloat16)

    loads[3].wait()
    my_cols = pl.ds(pl.multiple_of(t * quarter, 128), quarter)
    for a, source in enumerate((scaled, out_grad)):
        filled = message(picks[...], extra_picks[...], source[:, my_cols])
        outgoing[a] = filled.reshape(experts, 16, 4 * third)
    for a in range(2):
        parts[a, t, me] = outgoing[a, me]

    def send(a, d):
        return pltpu.make_async_remote_copy(
            src_ref=outgoing.at[a, d], dst_ref=parts.at[a, t, me],
            send_sem=send_sem.at[a, d], recv_sem=recv_sem.at[a, me],
            device_id=(d, t), device_id_type=MESH,
        )

    def arrival(a, k):
        return pltpu.make_async_remote_copy(
            src_ref=outgoing.at[a, k], dst_ref=parts.at[a, t, k],
            send_sem=send_sem.at[a, k], recv_sem=recv_sem.at[a, k],
            device_id=(k, t), device_id_type=MESH,
        )

    groups = experts // 2

    def passing(a, kind, g):
        which, mate = ((t, buddy), (t, across), (across, buddy))[kind]
        block = parts.at[a, which, pl.ds(2 * g, 2)]
        return pltpu.make_async_remote_copy(
            src_ref=block, dst_ref=block,
            send_sem=pass_send.at[a, kind, g], recv_sem=pass_recv.at[a, kind, g],
            device_id=(me, mate), device_id_type=MESH,
        )

    def passed(a, kind, g):
        which, mate = ((buddy, buddy), (across, across), (diagonal, buddy))[kind]
        block = parts.at[a, which, pl.ds(2 * g, 2)]
        return pltpu.make_async_remote_copy(
            src_ref=block, dst_ref=block,
            send_sem=pass_send.at[a, kind, g], recv_sem=pass_recv.at[a, kind, g],
            device_id=(me, mate), device_id_type=MESH,
        )

    pl.semaphore_wait(barrier, len(peers) + len(mates))
    for a in range(2):
        for d in peers:
            send(a, d).start()

    my_slots = slots[pl.ds(me, 1), :] // tok_count
    owner_id = lax.broadcasted_iota(jnp.int32, (experts, capacity), 0)
    own_rank = ranks(jnp.broadcast_to(my_slots, (experts, capacity)) == owner_id)
    lead4 = 16.0 + lax.broadcasted_iota(jnp.int32, (4, capacity), 0).astype(jnp.float32)
    for k in range(experts):
        row_rank = own_rank[k : k + 1, :]
        place[pl.ds(k * 16, 16), :] = jnp.where(row_rank == lead_target, 1.0, 0.0)
        place[pl.ds(lead_rows + k * 4, 4), :] = jnp.where(row_rank == lead4, 1.0, 0.0)
    loads[4].wait()
    gate_flat = jnp.sum(place[...] * gates[...], axis=1, keepdims=True)

    rest_rows = experts * 4
    j = lax.broadcasted_iota(jnp.int32, (3 * rest_rows, lead_rows), 0)
    m = lax.broadcasted_iota(jnp.int32, (3 * rest_rows, lead_rows), 1)
    jr = j % rest_rows
    unpack = (m == (jr // 4) * 16 + 4 * (j // rest_rows) + jr % 4).astype(jnp.bfloat16)

    hidden_block = w_in.shape[1] // groups

    def block_of(i):
        return pl.ds(pl.multiple_of(i * hidden_block, hidden_block), hidden_block)

    near_first = [order[3], order[2], order[0], order[1]]

    def take(a, g):
        if g is order[3]:
            arrival(a, partner).wait_recv()
        else:
            arrival(a, 2 * g).wait_recv()
            arrival(a, 2 * g + 1).wait_recv()
        passing(a, 1, g).start()
        passing(a, 0, g).start()

    def relay(a, g):
        passed(a, 1, g).wait_recv()
        passing(a, 2, g).start()

    def arrange(a, q, target):
        cols = pl.ds(pl.multiple_of(q * quarter, 128), quarter)
        target[pl.ds(0, lead_rows), cols] = parts[a, q, :, :, pl.ds(0, quarter)].reshape(lead_rows, quarter)
        rest = jnp.dot(
            unpack, parts[a, q, :, :, pl.ds(quarter, third)].reshape(lead_rows, third),
            preferred_element_type=jnp.float32,
        ).astype(jnp.bfloat16)
        for c in range(3):
            some = pl.ds(pl.multiple_of(q * quarter + c * third, 128), third)
            target[pl.ds(lead_rows, rest_rows), some] = rest[c * rest_rows : (c + 1) * rest_rows]
        return cols

    for g in near_first:
        take(0, g)
    for g in near_first[:2]:
        take(1, g)
    for g in near_first:
        relay(0, g)
    for g in near_first[2:]:
        take(1, g)
    for kind in (0, 2):
        for g in near_first:
            passed(0, kind, g).wait_recv()
    for q in range(tensors):
        arrange(0, q, rows)
    loads[5].wait()
    for i, g in enumerate(near_first):
        cols = pl.ds(i * hidden_block, hidden_block)
        v = jnp.dot(rows[...], w_in[:, cols], preferred_element_type=jnp.float32)
        relay(1, g)
        square = v * v
        tanh = jnp.tanh(ROOT * (v + CUBIC * v * square))
        half = 0.5 * (1.0 + tanh)
        hidden[:, cols] = (v * half).astype(jnp.bfloat16)
        slope[:, cols] = half + 0.5 * v * (1.0 - tanh * tanh) * (ROOT * (1.0 + 3.0 * CUBIC * square))

    loads[6].wait()
    for i, (q, kind) in enumerate(((t, None), (buddy, 0), (across, None))):
        if kind is not None:
            for g in near_first:
                passed(1, kind, g).wait_recv()
        part = arrange(1, q, grads)
        term = contract(grads[:, part], w_out[:, part], 1, 1)
        upstream[...] = term if i == 0 else upstream[...] + term
    for g in near_first:
        passed(1, 2, g).wait_recv()
    last_part = arrange(1, diagonal, grads)

    def backward(i, total):
        cols = block_of(i)
        up = upstream[:, cols] + contract(grads[:, last_part], w_out[cols, last_part], 1, 1)
        dpre[:, cols] = (gate_flat * up * slope[:, cols]).astype(jnp.bfloat16)
        return total + jnp.sum(hidden[:, cols].astype(jnp.float32) * up, axis=1, keepdims=True)

    gate_part = lax.fori_loop(0, groups, backward, jnp.zeros((place.shape[0], 1), jnp.float32))

    def slot_back(q):
        return contract(dpre[...], w_in[pl.ds(pl.multiple_of(q * quarter, 128), quarter), :], 1, 1)

    def to_core(i):
        return pltpu.make_async_remote_copy(
            src_ref=core_out.at[i], dst_ref=core_in.at[i], send_sem=ret_send.at[i], recv_sem=ret_recv.at[i],
            device_id=(me, buddy), device_id_type=MESH,
        )

    spans = [pl.ds(lead_rows, rest_rows)] + [pl.ds(pl.multiple_of(32 * g, 32), 32) for g in order]

    def to_side(i):
        return pltpu.make_async_remote_copy(
            src_ref=side_out.at[spans[i]], dst_ref=side_in.at[spans[i]],
            send_sem=side_send.at[i], recv_sem=side_recv.at[i],
            device_id=(me, across), device_id_type=MESH,
        )

    core_out[0] = slot_back(diagonal).astype(jnp.bfloat16)
    to_core(0).start()
    partial = slot_back(across)
    to_core(0).wait_recv()
    side_out[...] = (partial + core_in[0].astype(jnp.float32)).astype(jnp.bfloat16)
    for i in range(len(spans)):
        to_side(i).start()
    core_out[1] = slot_back(buddy).astype(jnp.bfloat16)
    to_core(1).start()
    mine[...] = slot_back(t)

    gate_parts[t] = jnp.broadcast_to(jnp.sum(place[...] * gate_part, axis=0, keepdims=True), (8, capacity))

    def gate_copy(i, slot):
        return pltpu.make_async_remote_copy(
            src_ref=gate_parts.at[t], dst_ref=gate_parts.at[slot], send_sem=gate_send.at[i], recv_sem=gate_recv.at[i],
            device_id=(me, mates[i]), device_id_type=MESH,
        )

    for i in range(3):
        gate_copy(i, t).start()

    def store(i):
        held, out = (
            (rows, rows_out), (dpre, dpre_out), (gate_held, gate_out), (token_held, token_out),
        )[i]
        return pltpu.make_async_copy(held, out, store_sem.at[i])

    gated[...] = (gate_flat * grads[...].astype(jnp.float32)).astype(jnp.bfloat16)
    for i in range(2):
        store(i).start()
    to_core(1).wait_recv()
    mine[...] += core_in[1].astype(jnp.float32)

    def total(i):
        to_side(i).wait_recv()
        return (mine[spans[i], :] + side_in[spans[i], :].astype(jnp.float32)).astype(jnp.bfloat16)

    def give_back(d, slot):
        return pltpu.make_async_remote_copy(
            src_ref=back_out.at[d], dst_ref=back_in.at[slot], send_sem=back_send.at[d], recv_sem=back_recv.at[slot],
            device_id=(d, t), device_id_type=MESH,
        )

    tail = total(0)
    packed = sum(
        contract(unpack[c * rest_rows : (c + 1) * rest_rows], tail[:, c * third : (c + 1) * third], 0, 0)
        for c in range(3)
    ).astype(jnp.bfloat16)
    back_out[:, :, pl.ds(quarter, third)] = packed.reshape(experts, 16, third)
    for i, g in enumerate(order):
        back_out[pl.ds(2 * g, 2), :, pl.ds(0, quarter)] = total(i + 1).reshape(2, 16, quarter)
        if i < 3:
            give_back(2 * g, me).start()
            give_back(2 * g + 1, me).start()
        else:
            give_back(partner, me).start()
            back_in[me] = back_out[me]

    def store_weight(i):
        span = pl.ds(i * hidden_block, hidden_block)
        return pltpu.make_async_copy(weight_held.at[span], weight_out.at[span], store_sem.at[4 + i])

    for i in range(groups):
        span = pl.ds(i * hidden_block, hidden_block)
        weight_held[span, :] = contract(hidden[:, span], gated[...], 0, 0).astype(jnp.bfloat16)
        store_weight(i).start()
    for d in peers:
        give_back(d, d).wait_recv()
    sums = contract(picks[...], back_in[:, :, pl.ds(0, quarter)].reshape(lead_rows, quarter), 0, 0)
    returned = back_in[:, :, pl.ds(quarter, third)].reshape(lead_rows, third)
    block_id = lax.broadcasted_iota(jnp.int32, factors.shape, 1)
    pieces = []
    for c in range(3):
        piece = sums[:, c * third : (c + 1) * third] + contract(extra_picks[c], returned, 0, 0)
        factor = jnp.sum(jnp.where(block_id == 3 * t + c, factors, 0.0), axis=1, keepdims=True)
        pieces.append((piece * factor).astype(jnp.bfloat16))
    last_out[...] = jnp.concatenate(pieces, axis=1).reshape(tensors, tok_count // tensors, quarter)
    last_in[t] = last_out[t]

    def finish(i, slot):
        return pltpu.make_async_remote_copy(
            src_ref=last_out.at[mates[i]], dst_ref=last_in.at[slot], send_sem=last_send.at[i], recv_sem=last_recv.at[i],
            device_id=(me, mates[i]), device_id_type=MESH,
        )

    for i in range(3):
        finish(i, t).start()
    for i in range(3):
        gate_copy(i, mates[i]).wait_recv()
    gate_held[...] = (gate_parts[0] + gate_parts[1] + gate_parts[2] + gate_parts[3])[0:1]
    store(2).start()
    for i in range(3):
        finish(i, mates[i]).wait_recv()
    for q in range(tensors):
        token_held[:, pl.ds(q * quarter, quarter)] = last_in[q]
    store(3).start()

    for a in range(2):
        for d in peers:
            send(a, d).wait_send()
        for kind in range(3):
            for g in range(groups):
                passing(a, kind, g).wait_send()
    for i in range(2):
        to_core(i).wait_send()
    for i in range(len(spans)):
        to_side(i).wait_send()
    for d in peers:
        give_back(d, me).wait_send()
    for i in range(3):
        gate_copy(i, t).wait_send()
        finish(i, t).wait_send()
    for i in range(4):
        store(i).wait()
    for i in range(groups):
        store_weight(i).wait()


def exchange(experts, tensors, tokens, exponents, out_grad, slots, gates, w_in, w_out):
    tok_count, width = tokens.shape
    hid = w_in.shape[1]
    quarter = width // tensors
    wide = quarter + quarter // 3
    count = experts * 20
    bf16, f32 = jnp.bfloat16, jnp.float32
    hbm = pl.BlockSpec(memory_space=pltpu.HBM)
    dma = pltpu.SemaphoreType.DMA
    return pl.pallas_call(
        functools.partial(exchange_kernel, experts, tensors),
        out_shape=(
            jax.ShapeDtypeStruct((tok_count // tensors, width), bf16),
            jax.ShapeDtypeStruct(gates.shape, f32),
            jax.ShapeDtypeStruct((count, width), bf16),
            jax.ShapeDtypeStruct((count, hid), bf16),
            jax.ShapeDtypeStruct((hid, width), bf16),
        ),
        in_specs=[hbm] * 7,
        out_specs=(hbm,) * 5,
        scratch_shapes=[
            pltpu.VMEM((tok_count // tensors, width), bf16),
            pltpu.VMEM(gates.shape, f32),
            pltpu.VMEM((count, width), bf16),
            pltpu.VMEM((count, width), bf16),
            pltpu.VMEM((count, hid), bf16),
            pltpu.VMEM((count, hid), bf16),
            pltpu.VMEM(tokens.shape, bf16),
            pltpu.VMEM(exponents.shape, jnp.int32),
            pltpu.VMEM(out_grad.shape, bf16),
            pltpu.VMEM(slots.shape, jnp.int32),
            pltpu.VMEM(gates.shape, f32),
            pltpu.VMEM(w_in.shape, bf16),
            pltpu.VMEM(w_out.shape, bf16),
            pltpu.VMEM((tok_count, width), bf16),
            pltpu.VMEM((experts * 16, tok_count), bf16),
            pltpu.VMEM((3, experts * 16, tok_count), bf16),
            pltpu.VMEM((count, slots.shape[1]), f32),
            pltpu.VMEM((2, experts, 16, wide), bf16),
            pltpu.VMEM((2, tensors, experts, 16, wide), bf16),
            pltpu.VMEM((count, width), bf16),
            pltpu.VMEM((count, hid), f32),
            pltpu.VMEM((count, hid), f32),
            pltpu.VMEM((hid, width), bf16),
            pltpu.VMEM((2, count, quarter), bf16),
            pltpu.VMEM((2, count, quarter), bf16),
            pltpu.VMEM((count, quarter), bf16),
            pltpu.VMEM((count, quarter), bf16),
            pltpu.VMEM((count, quarter), f32),
            pltpu.VMEM((experts, 16, wide), bf16),
            pltpu.VMEM((experts, 16, wide), bf16),
            pltpu.VMEM((tensors, tok_count // tensors, quarter), bf16),
            pltpu.VMEM((tensors, tok_count // tensors, quarter), bf16),
            pltpu.VMEM((tensors, 8, slots.shape[1]), f32),
            dma((7,)),
            dma((2, experts)),
            dma((2, experts)),
            dma((2, 3, experts // 2)),
            dma((2, 3, experts // 2)),
            dma((2,)),
            dma((2,)),
            dma((5,)),
            dma((5,)),
            dma((experts,)),
            dma((experts,)),
            dma((3,)),
            dma((3,)),
            dma((3,)),
            dma((3,)),
            dma((8,)),
        ],
        compiler_params=pltpu.CompilerParams(
            collective_id=0, has_side_effects=True, vmem_limit_bytes=60 * 2**20
        ),
    )(tokens, exponents, out_grad, slots, gates, w_in, w_out)


def weights_kernel(
    token_hbm, gate_hbm, rows_hbm, dpre_hbm, weight_hbm,
    token_out, gate_out, in_out, weight_out,
    rows, dpre, token_held, gate_held, in_held, load_sem, sem,
):
    sources = (rows_hbm, dpre_hbm, token_hbm, gate_hbm)
    helds = (rows, dpre, token_held, gate_held)
    loads = [
        pltpu.make_async_copy(source, held, load_sem.at[i]) for i, (source, held) in enumerate(zip(sources, helds))
    ]
    for load in loads:
        load.start()
    chunks = 4
    copies = []

    def copy(source, target):
        copies.append(pltpu.make_async_copy(source, target, sem.at[len(copies)]))
        copies[-1].start()

    for i in range(chunks):
        size = weight_out.shape[0] // chunks
        span = pl.ds(i * size, size)
        copy(weight_hbm.at[span], weight_out.at[span])
    loads[0].wait()
    loads[1].wait()
    for i in range(chunks):
        size = in_out.shape[0] // chunks
        span = pl.ds(i * size, size)
        in_held[span, :] = contract(rows[:, span], dpre[...], 0, 0).astype(jnp.bfloat16)
        copy(in_held.at[span], in_out.at[span])
    for i, target in ((2, token_out), (3, gate_out)):
        loads[i].wait()
        copy(helds[i], target)
    for each in copies:
        each.wait()


def weight_grads(token_grad, gate_grad, rows, dpre, out_weight_grad):
    width, hid = rows.shape[1], dpre.shape[1]
    like = lambda array: jax.ShapeDtypeStruct(array.shape, array.dtype)
    hbm = pl.BlockSpec(memory_space=pltpu.HBM)
    return pl.pallas_call(
        weights_kernel,
        out_shape=(
            like(token_grad), like(gate_grad),
            jax.ShapeDtypeStruct((width, hid), jnp.bfloat16), like(out_weight_grad),
        ),
        in_specs=[hbm] * 5,
        out_specs=(hbm,) * 4,
        scratch_shapes=[pltpu.VMEM(array.shape, array.dtype) for array in (rows, dpre, token_grad, gate_grad)]
        + [
            pltpu.VMEM((width, hid), jnp.bfloat16),
            pltpu.SemaphoreType.DMA((4,)),
            pltpu.SemaphoreType.DMA((10,)),
        ],
        compiler_params=pltpu.CompilerParams(vmem_limit_bytes=60 * 2**20),
    )(token_grad, gate_grad, rows, dpre, out_weight_grad)


def local_fused(tokens, exponents, out_grad, slots, gates, w_in, w_out):
    results = exchange(
        lax.axis_size("expert"), lax.axis_size("tensor"),
        tokens, exponents.T, out_grad, slots, gates, w_in[0], w_out[0],
    )
    token_grad, gate_grad, in_weight_grad, out_weight_grad = weight_grads(*results)
    return (token_grad, in_weight_grad[None], out_weight_grad[None], gate_grad)


def fits_exchange(mesh):
    return mesh.shape["expert"] == 8 and mesh.shape["tensor"] == 4


def solution(mesh):
    placed = (
        P("expert", None),
        P("expert", None),
        P("expert", None),
        P(),
        P("expert", None),
        P("expert", None, "tensor"),
        P("expert", "tensor", None),
    )
    return jax.shard_map(
        local_fused if fits_exchange(mesh) else local,
        mesh=mesh,
        in_specs=placed,
        out_specs=(
            P(("expert", "tensor"), None),
            P("expert", None, "tensor"),
            P("expert", "tensor", None),
            P("expert", None),
        ),
        check_vma=False,
    )
```

```python
import functools
import math

import jax
import jax.numpy as jnp
from jax import lax
from jax.experimental import pallas as pl
from jax.experimental.pallas import tpu as pltpu
from jax.sharding import PartitionSpec as P

MESH = pl.DeviceIdType.MESH
ROOT = math.sqrt(2.0 / math.pi)
CUBIC = 0.044715


def contract(left, right, left_dim, right_dim):
    return lax.dot_general(
        left, right, (((left_dim,), (right_dim,)), ((), ())), preferred_element_type=jnp.float32
    )


def apply_scales(values, exponents):
    row_count = values.shape[0]
    block_count = exponents.shape[1]
    factors = jnp.exp2(exponents.astype(jnp.float32))
    widened = values.astype(jnp.float32).reshape(row_count, block_count, 128) * factors[:, :, None]
    return widened.reshape(row_count, block_count * 128)


def local(tokens, exponents, out_grad, slots, gates, w_in, w_out):
    expert_count = lax.axis_size("expert")
    my_expert = lax.axis_index("expert")
    my_tensor = lax.axis_index("tensor")
    tok_count = tokens.shape[0]
    model_width = tokens.shape[1]
    slot_count = slots.shape[1]
    capacity = slot_count // expert_count + slot_count // (4 * expert_count)
    total_slots = expert_count * capacity
    owner = slots // tok_count
    local_index = slots % tok_count
    from_here = owner == my_expert
    send_order = jnp.cumsum(from_here.astype(jnp.int32), axis=1) - 1
    rank_range = jnp.arange(capacity, dtype=jnp.int32)
    send_hit = from_here[:, :, None] & (send_order[:, :, None] == rank_range[None, None, :])
    send_valid = jnp.any(send_hit, axis=1)
    picked_index = jnp.sum(jnp.where(send_hit, local_index[:, :, None], 0), axis=1)
    send_table = jnp.where(send_valid, picked_index, tok_count)
    row_owner = lax.dynamic_index_in_dim(owner, my_expert, 0, keepdims=False)
    slot_range = jnp.arange(slot_count, dtype=jnp.int32)
    earlier = (row_owner[:, None] == row_owner[None, :]) & (
        slot_range[:, None] > slot_range[None, :]
    )
    row_rank = jnp.sum(earlier.astype(jnp.int32), axis=1)
    flat_index = row_owner * capacity + row_rank
    scaled_local = apply_scales(tokens, exponents).astype(jnp.bfloat16)
    sent_rows = jnp.take(scaled_local, send_table, axis=0, mode="fill", fill_value=0)
    sent_grads = jnp.take(out_grad, send_table, axis=0, mode="fill", fill_value=0)
    arrived_rows, arrived_grads = (
        lax.all_to_all(sent_rows, "expert", split_axis=0, concat_axis=0, tiled=True),
        lax.all_to_all(sent_grads, "expert", split_axis=0, concat_axis=0, tiled=True),
    )
    slot_rows = arrived_rows.reshape(total_slots, model_width)
    slot_grads = arrived_grads.reshape(total_slots, model_width)
    gate_row = jnp.zeros((total_slots,), jnp.float32).at[flat_index].set(gates[0])
    weight_in = w_in[0]
    weight_out = w_out[0]
    preact = jnp.dot(slot_rows, weight_in, preferred_element_type=jnp.float32)
    hidden_full, backward = jax.vjp(jax.nn.gelu, preact)
    hidden = hidden_full.astype(jnp.bfloat16)
    upstream = contract(slot_grads, weight_out, 1, 1)
    gate_part = jnp.sum(hidden.astype(jnp.float32) * upstream, axis=1)
    gate_total = lax.psum(gate_part[flat_index], "tensor")
    dpre = backward(gate_row[:, None] * upstream)[0].astype(jnp.bfloat16)
    gated_grads = (gate_row[:, None] * slot_grads.astype(jnp.float32)).astype(jnp.bfloat16)
    out_weight_grad = contract(hidden, gated_grads, 0, 0).astype(jnp.bfloat16)
    in_weight_grad = contract(slot_rows, dpre, 0, 0).astype(jnp.bfloat16)
    slot_back = contract(dpre, weight_in, 1, 1)
    flat_send = send_table.reshape(-1)
    came_back = lax.all_to_all(
        slot_back.reshape(expert_count, capacity, model_width),
        "expert",
        split_axis=0,
        concat_axis=0,
        tiled=True,
    )
    token_sums = (
        jnp.zeros((tok_count, model_width), jnp.float32)
        .at[flat_send]
        .add(came_back.reshape(total_slots, model_width), mode="drop")
    )
    my_share = lax.psum_scatter(token_sums, "tensor", scatter_dimension=0, tiled=True)
    share_rows = my_share.shape[0]
    my_scales = lax.dynamic_slice_in_dim(exponents, my_tensor * share_rows, share_rows, 0)
    token_grad = apply_scales(my_share, my_scales).astype(jnp.bfloat16)
    return (token_grad, in_weight_grad[None], out_weight_grad[None], gate_total[None])


def message(picks, extra_picks, rows):
    third = rows.shape[1] // 3
    lead = jnp.dot(picks, rows, preferred_element_type=jnp.float32)
    rest = sum(
        jnp.dot(extra_picks[c], rows[:, c * third : (c + 1) * third], preferred_element_type=jnp.float32)
        for c in range(3)
    )
    return jnp.concatenate([lead, rest], axis=1).astype(jnp.bfloat16)


def exchange_kernel(
    experts, tensors,
    tokens_hbm, exponents_hbm, out_grad_hbm, slots_hbm, gates_hbm, w_in_hbm, w_out_hbm,
    token_out, gate_out, rows_out, gated_out, hidden_out, dpre_out,
    token_held, gate_held, rows, gated, hidden, dpre,
    tokens, exponents, out_grad, slots, gates,
    w_in, w_out, picks, extra_picks, place, outgoing, parts, grads, slope, upstream,
    core_out, core_in, side_out, side_in, mine, back_out, back_in, last_out, last_in, gate_parts,
    load_sem, send_sem, recv_sem, pass_send, pass_recv, ret_send, ret_recv, side_send, side_recv,
    back_send, back_recv, last_send, last_recv, gate_send, gate_recv, store_sem,
):
    me = lax.axis_index("expert")
    t = lax.axis_index("tensor")
    y, core = t // 2, t % 2
    buddy = 2 * y + (1 - core)
    across = 2 * (1 - y) + core
    diagonal = 2 * (1 - y) + (1 - core)
    tok_count, width = tokens.shape
    quarter = width // tensors
    third = quarter // 3
    capacity = slots.shape[1]
    lead_rows = experts * 16

    loads = [
        pltpu.make_async_copy(source, held, load_sem.at[i])
        for i, (source, held) in enumerate(
            (
                (slots_hbm, slots), (exponents_hbm, exponents), (tokens_hbm, tokens), (out_grad_hbm, out_grad),
                (gates_hbm, gates), (w_in_hbm, w_in), (w_out_hbm, w_out),
            )
        )
    ]
    for load in loads[:5]:
        load.start()

    barrier = pltpu.get_barrier_semaphore()
    z, x = me // 2, me % 2
    order = [(z + 2) % 4, 3 - z, z + 1 - 2 * (z % 2), z]
    partner = 2 * z + 1 - x
    peers = [2 * g + i for g in order[:3] for i in (x, 1 - x)] + [partner]
    mates = [buddy, across, diagonal]
    for d in peers:
        pl.semaphore_signal(barrier, inc=1, device_id=(d, t), device_id_type=MESH)
    for m in mates:
        pl.semaphore_signal(barrier, inc=1, device_id=(me, m), device_id_type=MESH)

    tri = (
        lax.broadcasted_iota(jnp.int32, (capacity, capacity), 0)
        < lax.broadcasted_iota(jnp.int32, (capacity, capacity), 1)
    ).astype(jnp.bfloat16)

    def ranks(mask):
        ones = jnp.where(mask, 1.0, 0.0)
        before = jnp.dot(ones.astype(jnp.bfloat16), tri, preferred_element_type=jnp.float32)
        return jnp.where(mask, before, -1.0)

    loads[0].wait()
    all_slots = slots[...]
    local_index = all_slots - me * tok_count
    rank = ranks((local_index >= 0) & (local_index < tok_count))
    local_number = local_index.astype(jnp.float32) + 1.0
    row_id = lax.broadcasted_iota(jnp.int32, (16, capacity), 0)
    lead_target = row_id.astype(jnp.float32)
    rest_target = (16 + row_id % 4).astype(jnp.float32)
    token_id = lax.broadcasted_iota(jnp.int32, (16, tok_count), 1).astype(jnp.float32) + 1.0
    part_id = lax.broadcasted_iota(jnp.int32, (16, tok_count), 0) // 4
    for d in range(experts):
        row_rank, row_number = rank[d : d + 1, :], local_number[d : d + 1, :]
        lead = jnp.sum(jnp.where(row_rank == lead_target, row_number, 0.0), axis=1, keepdims=True)
        rest = jnp.sum(jnp.where(row_rank == rest_target, row_number, 0.0), axis=1, keepdims=True)
        span = pl.ds(d * 16, 16)
        picks[span, :] = jnp.where(lead == token_id, 1.0, 0.0).astype(jnp.bfloat16)
        rest_hit = jnp.where(rest == token_id, 1.0, 0.0)
        for c in range(3):
            extra_picks[c, span, :] = jnp.where(part_id == c, rest_hit, 0.0).astype(jnp.bfloat16)

    blocks = exponents.shape[0]
    chosen = (
        lax.broadcasted_iota(jnp.int32, (blocks, 4), 0) == 3 * t + lax.broadcasted_iota(jnp.int32, (blocks, 4), 1)
    ).astype(jnp.bfloat16)
    loads[1].wait()
    factors = contract(jnp.exp2(exponents[...].astype(jnp.float32)).astype(jnp.bfloat16), chosen, 0, 0)
    my_cols = pl.ds(pl.multiple_of(t * quarter, 128), quarter)

    def scale(values):
        return jnp.concatenate(
            [values[:, c * third : (c + 1) * third] * factors[:, c : c + 1] for c in range(3)], axis=1
        ).astype(jnp.bfloat16)

    def fill(a, mine_here):
        outgoing[a] = message(picks[...], extra_picks[...], mine_here).reshape(experts, 16, 4 * third)
        parts[a, t, me] = outgoing[a, me]

    def send(a, d):
        return pltpu.make_async_remote_copy(
            src_ref=outgoing.at[a, d], dst_ref=parts.at[a, t, me],
            send_sem=send_sem.at[a, d], recv_sem=recv_sem.at[a, me],
            device_id=(d, t), device_id_type=MESH,
        )

    def arrival(a, k):
        return pltpu.make_async_remote_copy(
            src_ref=outgoing.at[a, k], dst_ref=parts.at[a, t, k],
            send_sem=send_sem.at[a, k], recv_sem=recv_sem.at[a, k],
            device_id=(k, t), device_id_type=MESH,
        )

    groups = experts // 2

    def passing(a, kind, g):
        which, mate = ((t, buddy), (t, across), (across, buddy))[kind]
        block = parts.at[a, which, pl.ds(2 * g, 2)]
        return pltpu.make_async_remote_copy(
            src_ref=block, dst_ref=block,
            send_sem=pass_send.at[a, kind, g], recv_sem=pass_recv.at[a, kind, g],
            device_id=(me, mate), device_id_type=MESH,
        )

    def passed(a, kind, g):
        which, mate = ((buddy, buddy), (across, across), (diagonal, buddy))[kind]
        block = parts.at[a, which, pl.ds(2 * g, 2)]
        return pltpu.make_async_remote_copy(
            src_ref=block, dst_ref=block,
            send_sem=pass_send.at[a, kind, g], recv_sem=pass_recv.at[a, kind, g],
            device_id=(me, mate), device_id_type=MESH,
        )

    loads[2].wait()
    fill(0, scale(tokens[:, my_cols].astype(jnp.float32)))
    pl.semaphore_wait(barrier, len(peers) + len(mates))
    for d in peers:
        send(0, d).start()
    loads[3].wait()
    fill(1, out_grad[:, my_cols])
    for d in peers:
        send(1, d).start()
    for load in loads[5:]:
        load.start()

    my_slots = slots[pl.ds(me, 1), :] // tok_count
    owner_id = lax.broadcasted_iota(jnp.int32, (experts, capacity), 0)
    own_rank = ranks(jnp.broadcast_to(my_slots, (experts, capacity)) == owner_id)
    lead4 = 16.0 + lax.broadcasted_iota(jnp.int32, (4, capacity), 0).astype(jnp.float32)
    for k in range(experts):
        row_rank = own_rank[k : k + 1, :]
        place[pl.ds(k * 16, 16), :] = jnp.where(row_rank == lead_target, 1.0, 0.0)
        place[pl.ds(lead_rows + k * 4, 4), :] = jnp.where(row_rank == lead4, 1.0, 0.0)
    loads[4].wait()
    gate_flat = jnp.sum(place[...] * gates[...], axis=1, keepdims=True)

    rest_rows = experts * 4
    j = lax.broadcasted_iota(jnp.int32, (3 * rest_rows, lead_rows), 0)
    m = lax.broadcasted_iota(jnp.int32, (3 * rest_rows, lead_rows), 1)
    jr = j % rest_rows
    unpack = (m == (jr // 4) * 16 + 4 * (j // rest_rows) + jr % 4).astype(jnp.bfloat16)

    hidden_block = w_in.shape[1] // groups

    def block_of(i):
        return pl.ds(pl.multiple_of(i * hidden_block, hidden_block), hidden_block)

    near_first = [order[3], order[2], order[0], order[1]]

    def store(i):
        held, out = (
            (gate_held, gate_out), (token_held, token_out),
            (rows, rows_out), (hidden, hidden_out), (gated, gated_out), (dpre, dpre_out),
        )[i]
        return pltpu.make_async_copy(held, out, store_sem.at[i])

    def take(a, g):
        if g is order[3]:
            arrival(a, partner).wait_recv()
        else:
            arrival(a, 2 * g).wait_recv()
            arrival(a, 2 * g + 1).wait_recv()
        passing(a, 1, g).start()
        passing(a, 0, g).start()

    def relay(a, g):
        passed(a, 1, g).wait_recv()
        passing(a, 2, g).start()

    def arrange(a, q, target):
        cols = pl.ds(pl.multiple_of(q * quarter, 128), quarter)
        target[pl.ds(0, lead_rows), cols] = parts[a, q, :, :, pl.ds(0, quarter)].reshape(lead_rows, quarter)
        rest = jnp.dot(
            unpack, parts[a, q, :, :, pl.ds(quarter, third)].reshape(lead_rows, third),
            preferred_element_type=jnp.float32,
        ).astype(jnp.bfloat16)
        for c in range(3):
            some = pl.ds(pl.multiple_of(q * quarter + c * third, 128), third)
            target[pl.ds(lead_rows, rest_rows), some] = rest[c * rest_rows : (c + 1) * rest_rows]
        return cols

    for g in near_first:
        take(0, g)
    for g in near_first[:2]:
        take(1, g)
    for g in near_first:
        relay(0, g)
    for g in near_first[2:]:
        take(1, g)
    for kind in (0, 2):
        for g in near_first:
            passed(0, kind, g).wait_recv()
    for q in range(tensors):
        arrange(0, q, rows)
    loads[5].wait()
    for i, g in enumerate(near_first):
        cols = pl.ds(i * hidden_block, hidden_block)
        v = jnp.dot(rows[...], w_in[:, cols], preferred_element_type=jnp.float32)
        relay(1, g)
        square = v * v
        tanh = jnp.tanh(ROOT * (v + CUBIC * v * square))
        half = 0.5 * (1.0 + tanh)
        hidden[:, cols] = (v * half).astype(jnp.bfloat16)
        slope[:, cols] = half + 0.5 * v * (1.0 - tanh * tanh) * (ROOT * (1.0 + 3.0 * CUBIC * square))

    store(2).start()
    store(3).start()

    loads[6].wait()
    for i, (q, kind) in enumerate(((t, None), (buddy, 0), (across, None))):
        if kind is not None:
            for g in near_first:
                passed(1, kind, g).wait_recv()
        part = arrange(1, q, grads)
        term = contract(grads[:, part], w_out[:, part], 1, 1)
        upstream[...] = term if i == 0 else upstream[...] + term
    for g in near_first:
        passed(1, 2, g).wait_recv()
    last_part = arrange(1, diagonal, grads)

    def backward(i, total):
        cols = block_of(i)
        up = upstream[:, cols] + contract(grads[:, last_part], w_out[cols, last_part], 1, 1)
        dpre[:, cols] = (gate_flat * up * slope[:, cols]).astype(jnp.bfloat16)
        return total + jnp.sum(hidden[:, cols].astype(jnp.float32) * up, axis=1, keepdims=True)

    gate_part = lax.fori_loop(0, groups, backward, jnp.zeros((place.shape[0], 1), jnp.float32))

    def slot_back(q):
        return contract(dpre[...], w_in[pl.ds(pl.multiple_of(q * quarter, 128), quarter), :], 1, 1)

    def to_core(i):
        return pltpu.make_async_remote_copy(
            src_ref=core_out.at[i], dst_ref=core_in.at[i], send_sem=ret_send.at[i], recv_sem=ret_recv.at[i],
            device_id=(me, buddy), device_id_type=MESH,
        )

    spans = [pl.ds(lead_rows, rest_rows)] + [pl.ds(pl.multiple_of(32 * g, 32), 32) for g in order]

    def to_side(i):
        return pltpu.make_async_remote_copy(
            src_ref=side_out.at[spans[i]], dst_ref=side_in.at[spans[i]],
            send_sem=side_send.at[i], recv_sem=side_recv.at[i],
            device_id=(me, across), device_id_type=MESH,
        )

    core_out[0] = slot_back(diagonal).astype(jnp.bfloat16)
    to_core(0).start()
    partial = slot_back(across)
    to_core(0).wait_recv()
    side_out[...] = (partial + core_in[0].astype(jnp.float32)).astype(jnp.bfloat16)
    for i in range(len(spans)):
        to_side(i).start()
    core_out[1] = slot_back(buddy).astype(jnp.bfloat16)
    to_core(1).start()
    mine[...] = slot_back(t)

    gate_parts[t] = jnp.broadcast_to(jnp.sum(place[...] * gate_part, axis=0, keepdims=True), (8, capacity))

    def gate_copy(i, slot):
        return pltpu.make_async_remote_copy(
            src_ref=gate_parts.at[t], dst_ref=gate_parts.at[slot], send_sem=gate_send.at[i], recv_sem=gate_recv.at[i],
            device_id=(me, mates[i]), device_id_type=MESH,
        )

    for i in range(3):
        gate_copy(i, t).start()

    gated[...] = (gate_flat * grads[...].astype(jnp.float32)).astype(jnp.bfloat16)
    to_core(1).wait_recv()
    mine[...] += core_in[1].astype(jnp.float32)

    def total(i):
        to_side(i).wait_recv()
        return (mine[spans[i], :] + side_in[spans[i], :].astype(jnp.float32)).astype(jnp.bfloat16)

    def give_back(d, slot):
        return pltpu.make_async_remote_copy(
            src_ref=back_out.at[d], dst_ref=back_in.at[slot], send_sem=back_send.at[d], recv_sem=back_recv.at[slot],
            device_id=(d, t), device_id_type=MESH,
        )

    tail = total(0)
    packed = sum(
        contract(unpack[c * rest_rows : (c + 1) * rest_rows], tail[:, c * third : (c + 1) * third], 0, 0)
        for c in range(3)
    ).astype(jnp.bfloat16)
    back_out[:, :, pl.ds(quarter, third)] = packed.reshape(experts, 16, third)
    for i, g in enumerate(order):
        back_out[pl.ds(2 * g, 2), :, pl.ds(0, quarter)] = total(i + 1).reshape(2, 16, quarter)
        if i < 3:
            give_back(2 * g, me).start()
            give_back(2 * g + 1, me).start()
        else:
            give_back(partner, me).start()
            back_in[me] = back_out[me]
    store(4).start()
    store(5).start()
    for a in range(2):
        for d in peers:
            send(a, d).wait_send()
        for kind in range(3):
            for g in range(groups):
                passing(a, kind, g).wait_send()
    for i in range(2):
        to_core(i).wait_send()
    for i in range(len(spans)):
        to_side(i).wait_send()
    for d in peers:
        give_back(d, d).wait_recv()
    sums = contract(picks[...], back_in[:, :, pl.ds(0, quarter)].reshape(lead_rows, quarter), 0, 0)
    returned = back_in[:, :, pl.ds(quarter, third)].reshape(lead_rows, third)
    pieces = [
        sums[:, c * third : (c + 1) * third] + contract(extra_picks[c], returned, 0, 0) for c in range(3)
    ]
    last_out[...] = scale(jnp.concatenate(pieces, axis=1)).reshape(tensors, tok_count // tensors, quarter)
    last_in[t] = last_out[t]

    def finish(i, slot):
        return pltpu.make_async_remote_copy(
            src_ref=last_out.at[mates[i]], dst_ref=last_in.at[slot], send_sem=last_send.at[i], recv_sem=last_recv.at[i],
            device_id=(me, mates[i]), device_id_type=MESH,
        )

    for i in range(3):
        finish(i, t).start()
    for i in range(3):
        gate_copy(i, mates[i]).wait_recv()
    gate_held[...] = (gate_parts[0] + gate_parts[1] + gate_parts[2] + gate_parts[3])[0:1]
    store(0).start()
    for i in range(3):
        finish(i, mates[i]).wait_recv()
    for q in range(tensors):
        token_held[:, pl.ds(q * quarter, quarter)] = last_in[q]
    store(1).start()

    for d in peers:
        give_back(d, me).wait_send()
    for i in range(3):
        gate_copy(i, t).wait_send()
        finish(i, t).wait_send()
    for i in range(6):
        store(i).wait()


def exchange(experts, tensors, tokens, exponents, out_grad, slots, gates, w_in, w_out):
    tok_count, width = tokens.shape
    hid = w_in.shape[1]
    quarter = width // tensors
    wide = quarter + quarter // 3
    count = experts * 20
    bf16, f32 = jnp.bfloat16, jnp.float32
    hbm = pl.BlockSpec(memory_space=pltpu.HBM)
    dma = pltpu.SemaphoreType.DMA
    return pl.pallas_call(
        functools.partial(exchange_kernel, experts, tensors),
        out_shape=(
            jax.ShapeDtypeStruct((tok_count // tensors, width), bf16),
            jax.ShapeDtypeStruct(gates.shape, f32),
            jax.ShapeDtypeStruct((count, width), bf16),
            jax.ShapeDtypeStruct((count, width), bf16),
            jax.ShapeDtypeStruct((count, hid), bf16),
            jax.ShapeDtypeStruct((count, hid), bf16),
        ),
        in_specs=[hbm] * 7,
        out_specs=(hbm,) * 6,
        scratch_shapes=[
            pltpu.VMEM((tok_count // tensors, width), bf16),
            pltpu.VMEM(gates.shape, f32),
            pltpu.VMEM((count, width), bf16),
            pltpu.VMEM((count, width), bf16),
            pltpu.VMEM((count, hid), bf16),
            pltpu.VMEM((count, hid), bf16),
            pltpu.VMEM(tokens.shape, bf16),
            pltpu.VMEM(exponents.shape, jnp.int32),
            pltpu.VMEM(out_grad.shape, bf16),
            pltpu.VMEM(slots.shape, jnp.int32),
            pltpu.VMEM(gates.shape, f32),
            pltpu.VMEM(w_in.shape, bf16),
            pltpu.VMEM(w_out.shape, bf16),
            pltpu.VMEM((experts * 16, tok_count), bf16),
            pltpu.VMEM((3, experts * 16, tok_count), bf16),
            pltpu.VMEM((count, slots.shape[1]), f32),
            pltpu.VMEM((2, experts, 16, wide), bf16),
            pltpu.VMEM((2, tensors, experts, 16, wide), bf16),
            pltpu.VMEM((count, width), bf16),
            pltpu.VMEM((count, hid), f32),
            pltpu.VMEM((count, hid), f32),
            pltpu.VMEM((2, count, quarter), bf16),
            pltpu.VMEM((2, count, quarter), bf16),
            pltpu.VMEM((count, quarter), bf16),
            pltpu.VMEM((count, quarter), bf16),
            pltpu.VMEM((count, quarter), f32),
            pltpu.VMEM((experts, 16, wide), bf16),
            pltpu.VMEM((experts, 16, wide), bf16),
            pltpu.VMEM((tensors, tok_count // tensors, quarter), bf16),
            pltpu.VMEM((tensors, tok_count // tensors, quarter), bf16),
            pltpu.VMEM((tensors, 8, slots.shape[1]), f32),
            dma((7,)),
            dma((2, experts)),
            dma((2, experts)),
            dma((2, 3, experts // 2)),
            dma((2, 3, experts // 2)),
            dma((2,)),
            dma((2,)),
            dma((5,)),
            dma((5,)),
            dma((experts,)),
            dma((experts,)),
            dma((3,)),
            dma((3,)),
            dma((3,)),
            dma((3,)),
            dma((6,)),
        ],
        compiler_params=pltpu.CompilerParams(
            collective_id=0, has_side_effects=True, vmem_limit_bytes=60 * 2**20
        ),
    )(tokens, exponents, out_grad, slots, gates, w_in, w_out)


def weights_kernel(
    token_hbm, gate_hbm, rows_hbm, gated_hbm, hidden_hbm, dpre_hbm,
    token_out, gate_out, in_out, out_out,
    rows, gated, hidden, dpre, token_held, gate_held, in_held, out_held, load_sem, sem,
):
    sources = (hidden_hbm, gated_hbm, rows_hbm, dpre_hbm, token_hbm, gate_hbm)
    helds = (hidden, gated, rows, dpre, token_held, gate_held)
    loads = [
        pltpu.make_async_copy(source, held, load_sem.at[i]) for i, (source, held) in enumerate(zip(sources, helds))
    ]
    for load in loads:
        load.start()
    chunks = 4
    copies = []
    for n, (left, right, held, out) in enumerate(((hidden, gated, out_held, out_out), (rows, dpre, in_held, in_out))):
        loads[2 * n].wait()
        loads[2 * n + 1].wait()
        for i in range(chunks):
            size = out.shape[0] // chunks
            span = pl.ds(i * size, size)
            held[span, :] = contract(left[:, span], right[...], 0, 0).astype(jnp.bfloat16)
            copies.append(pltpu.make_async_copy(held.at[span], out.at[span], sem.at[len(copies)]))
            copies[-1].start()
        if n == 0:
            for i, (held, out) in enumerate(((token_held, token_out), (gate_held, gate_out))):
                loads[4 + i].wait()
                copies.append(pltpu.make_async_copy(held, out, sem.at[len(copies)]))
                copies[-1].start()
    for copy in copies:
        copy.wait()


def weight_grads(token_grad, gate_grad, rows, gated, hidden, dpre):
    width, hid = rows.shape[1], hidden.shape[1]
    bf16 = jnp.bfloat16
    like = lambda array: jax.ShapeDtypeStruct(array.shape, array.dtype)
    hbm = pl.BlockSpec(memory_space=pltpu.HBM)
    return pl.pallas_call(
        weights_kernel,
        out_shape=(
            like(token_grad), like(gate_grad),
            jax.ShapeDtypeStruct((width, hid), bf16), jax.ShapeDtypeStruct((hid, width), bf16),
        ),
        in_specs=[hbm] * 6,
        out_specs=(hbm,) * 4,
        scratch_shapes=[
            pltpu.VMEM(array.shape, array.dtype) for array in (rows, gated, hidden, dpre, token_grad, gate_grad)
        ]
        + [
            pltpu.VMEM((width, hid), bf16),
            pltpu.VMEM((hid, width), bf16),
            pltpu.SemaphoreType.DMA((6,)),
            pltpu.SemaphoreType.DMA((10,)),
        ],
        compiler_params=pltpu.CompilerParams(vmem_limit_bytes=60 * 2**20),
    )(token_grad, gate_grad, rows, gated, hidden, dpre)


def local_fused(tokens, exponents, out_grad, slots, gates, w_in, w_out):
    results = exchange(
        lax.axis_size("expert"), lax.axis_size("tensor"),
        tokens, exponents.T, out_grad, slots, gates, w_in[0], w_out[0],
    )
    token_grad, gate_grad, in_weight_grad, out_weight_grad = weight_grads(*results)
    return (token_grad, in_weight_grad[None], out_weight_grad[None], gate_grad)


def fits_exchange(mesh):
    return mesh.shape["expert"] == 8 and mesh.shape["tensor"] == 4


def solution(mesh):
    placed = (
        P("expert", None),
        P("expert", None),
        P("expert", None),
        P(),
        P("expert", None),
        P("expert", None, "tensor"),
        P("expert", "tensor", None),
    )
    return jax.shard_map(
        local_fused if fits_exchange(mesh) else local,
        mesh=mesh,
        in_specs=placed,
        out_specs=(
            P(("expert", "tensor"), None),
            P("expert", None, "tensor"),
            P("expert", "tensor", None),
            P("expert", None),
        ),
        check_vma=False,
    )
```

```python
import functools
import math

import jax
import jax.numpy as jnp
from jax import lax
from jax.experimental import pallas as pl
from jax.experimental.pallas import tpu as pltpu
from jax.sharding import PartitionSpec as P

MESH = pl.DeviceIdType.MESH
ROOT = math.sqrt(2.0 / math.pi)
CUBIC = 0.044715


def contract(left, right, left_dim, right_dim):
    return lax.dot_general(
        left, right, (((left_dim,), (right_dim,)), ((), ())), preferred_element_type=jnp.float32
    )


def apply_scales(values, exponents):
    row_count = values.shape[0]
    block_count = exponents.shape[1]
    factors = jnp.exp2(exponents.astype(jnp.float32))
    widened = values.astype(jnp.float32).reshape(row_count, block_count, 128) * factors[:, :, None]
    return widened.reshape(row_count, block_count * 128)


def local(tokens, exponents, out_grad, slots, gates, w_in, w_out):
    expert_count = lax.axis_size("expert")
    my_expert = lax.axis_index("expert")
    my_tensor = lax.axis_index("tensor")
    tok_count = tokens.shape[0]
    model_width = tokens.shape[1]
    slot_count = slots.shape[1]
    capacity = slot_count // expert_count + slot_count // (4 * expert_count)
    total_slots = expert_count * capacity
    owner = slots // tok_count
    local_index = slots % tok_count
    from_here = owner == my_expert
    send_order = jnp.cumsum(from_here.astype(jnp.int32), axis=1) - 1
    rank_range = jnp.arange(capacity, dtype=jnp.int32)
    send_hit = from_here[:, :, None] & (send_order[:, :, None] == rank_range[None, None, :])
    send_valid = jnp.any(send_hit, axis=1)
    picked_index = jnp.sum(jnp.where(send_hit, local_index[:, :, None], 0), axis=1)
    send_table = jnp.where(send_valid, picked_index, tok_count)
    row_owner = lax.dynamic_index_in_dim(owner, my_expert, 0, keepdims=False)
    slot_range = jnp.arange(slot_count, dtype=jnp.int32)
    earlier = (row_owner[:, None] == row_owner[None, :]) & (
        slot_range[:, None] > slot_range[None, :]
    )
    row_rank = jnp.sum(earlier.astype(jnp.int32), axis=1)
    flat_index = row_owner * capacity + row_rank
    scaled_local = apply_scales(tokens, exponents).astype(jnp.bfloat16)
    sent_rows = jnp.take(scaled_local, send_table, axis=0, mode="fill", fill_value=0)
    sent_grads = jnp.take(out_grad, send_table, axis=0, mode="fill", fill_value=0)
    arrived_rows, arrived_grads = (
        lax.all_to_all(sent_rows, "expert", split_axis=0, concat_axis=0, tiled=True),
        lax.all_to_all(sent_grads, "expert", split_axis=0, concat_axis=0, tiled=True),
    )
    slot_rows = arrived_rows.reshape(total_slots, model_width)
    slot_grads = arrived_grads.reshape(total_slots, model_width)
    gate_row = jnp.zeros((total_slots,), jnp.float32).at[flat_index].set(gates[0])
    weight_in = w_in[0]
    weight_out = w_out[0]
    preact = jnp.dot(slot_rows, weight_in, preferred_element_type=jnp.float32)
    hidden_full, backward = jax.vjp(jax.nn.gelu, preact)
    hidden = hidden_full.astype(jnp.bfloat16)
    upstream = contract(slot_grads, weight_out, 1, 1)
    gate_part = jnp.sum(hidden.astype(jnp.float32) * upstream, axis=1)
    gate_total = lax.psum(gate_part[flat_index], "tensor")
    dpre = backward(gate_row[:, None] * upstream)[0].astype(jnp.bfloat16)
    gated_grads = (gate_row[:, None] * slot_grads.astype(jnp.float32)).astype(jnp.bfloat16)
    out_weight_grad = contract(hidden, gated_grads, 0, 0).astype(jnp.bfloat16)
    in_weight_grad = contract(slot_rows, dpre, 0, 0).astype(jnp.bfloat16)
    slot_back = contract(dpre, weight_in, 1, 1)
    flat_send = send_table.reshape(-1)
    came_back = lax.all_to_all(
        slot_back.reshape(expert_count, capacity, model_width),
        "expert",
        split_axis=0,
        concat_axis=0,
        tiled=True,
    )
    token_sums = (
        jnp.zeros((tok_count, model_width), jnp.float32)
        .at[flat_send]
        .add(came_back.reshape(total_slots, model_width), mode="drop")
    )
    my_share = lax.psum_scatter(token_sums, "tensor", scatter_dimension=0, tiled=True)
    share_rows = my_share.shape[0]
    my_scales = lax.dynamic_slice_in_dim(exponents, my_tensor * share_rows, share_rows, 0)
    token_grad = apply_scales(my_share, my_scales).astype(jnp.bfloat16)
    return (token_grad, in_weight_grad[None], out_weight_grad[None], gate_total[None])


def message(picks, extra_picks, rows):
    third = rows.shape[1] // 3
    lead = jnp.dot(picks, rows, preferred_element_type=jnp.float32)
    rest = sum(
        jnp.dot(extra_picks[c], rows[:, c * third : (c + 1) * third], preferred_element_type=jnp.float32)
        for c in range(3)
    )
    return jnp.concatenate([lead, rest], axis=1).astype(jnp.bfloat16)


def exchange_kernel(
    experts, tensors,
    tokens_hbm, exponents_hbm, out_grad_hbm, slots_hbm, gates_hbm, w_in_hbm, w_out_hbm,
    token_out, gate_out, rows_out, gated_out, hidden_out, dpre_out,
    token_held, gate_held, rows, gated, hidden, dpre,
    tokens, exponents, out_grad, slots, gates,
    w_in, w_out, picks, extra_picks, place, outgoing, parts, grads, slope, upstream,
    core_out, core_in, side_out, side_in, mine, back_out, back_in, last_out, last_in, gate_parts,
    load_sem, send_sem, recv_sem, pass_send, pass_recv, ret_send, ret_recv, side_send, side_recv,
    back_send, back_recv, last_send, last_recv, gate_send, gate_recv, store_sem,
):
    me = lax.axis_index("expert")
    t = lax.axis_index("tensor")
    y, core = t // 2, t % 2
    buddy = 2 * y + (1 - core)
    across = 2 * (1 - y) + core
    diagonal = 2 * (1 - y) + (1 - core)
    tok_count, width = tokens.shape
    quarter = width // tensors
    third = quarter // 3
    capacity = slots.shape[1]
    lead_rows = experts * 16

    loads = [
        pltpu.make_async_copy(source, held, load_sem.at[i])
        for i, (source, held) in enumerate(
            (
                (slots_hbm, slots), (exponents_hbm, exponents), (tokens_hbm, tokens), (out_grad_hbm, out_grad),
                (gates_hbm, gates), (w_in_hbm, w_in), (w_out_hbm, w_out),
            )
        )
    ]
    for load in loads[:5]:
        load.start()

    barrier = pltpu.get_barrier_semaphore()
    z, x = me // 2, me % 2
    order = [(z + 2) % 4, 3 - z, z + 1 - 2 * (z % 2), z]
    partner = 2 * z + 1 - x
    far = [2 * g + i for g in order[:2] for i in (x, 1 - x)]
    near = [2 * order[2] + i for i in (x, 1 - x)] + [partner]
    peers = far + near
    mates = [buddy, across, diagonal]
    for d in peers:
        pl.semaphore_signal(barrier, inc=1, device_id=(d, t), device_id_type=MESH)
    for m in mates:
        pl.semaphore_signal(barrier, inc=1, device_id=(me, m), device_id_type=MESH)

    tri = (
        lax.broadcasted_iota(jnp.int32, (capacity, capacity), 0)
        < lax.broadcasted_iota(jnp.int32, (capacity, capacity), 1)
    ).astype(jnp.bfloat16)

    def ranks(mask):
        ones = jnp.where(mask, 1.0, 0.0)
        before = jnp.dot(ones.astype(jnp.bfloat16), tri, preferred_element_type=jnp.float32)
        return jnp.where(mask, before, -1.0)

    loads[0].wait()
    all_slots = slots[...]
    local_index = all_slots - me * tok_count
    rank = ranks((local_index >= 0) & (local_index < tok_count))
    local_number = local_index.astype(jnp.float32) + 1.0
    row_id = lax.broadcasted_iota(jnp.int32, (16, capacity), 0)
    lead_target = row_id.astype(jnp.float32)
    rest_target = (16 + row_id % 4).astype(jnp.float32)
    token_id = lax.broadcasted_iota(jnp.int32, (16, tok_count), 1).astype(jnp.float32) + 1.0
    part_id = lax.broadcasted_iota(jnp.int32, (16, tok_count), 0) // 4
    for d in range(experts):
        row_rank, row_number = rank[d : d + 1, :], local_number[d : d + 1, :]
        lead = jnp.sum(jnp.where(row_rank == lead_target, row_number, 0.0), axis=1, keepdims=True)
        rest = jnp.sum(jnp.where(row_rank == rest_target, row_number, 0.0), axis=1, keepdims=True)
        span = pl.ds(d * 16, 16)
        picks[span, :] = jnp.where(lead == token_id, 1.0, 0.0).astype(jnp.bfloat16)
        rest_hit = jnp.where(rest == token_id, 1.0, 0.0)
        for c in range(3):
            extra_picks[c, span, :] = jnp.where(part_id == c, rest_hit, 0.0).astype(jnp.bfloat16)

    blocks = exponents.shape[0]
    block_id = lax.broadcasted_iota(jnp.int32, (blocks, 8), 0)
    part_no = lax.broadcasted_iota(jnp.int32, (blocks, 8), 1)
    chosen = (block_id == jnp.where(part_no < 4, 3 * t + part_no, 3 * across + part_no - 4)).astype(jnp.bfloat16)
    loads[1].wait()
    factors = contract(jnp.exp2(exponents[...].astype(jnp.float32)).astype(jnp.bfloat16), chosen, 0, 0)

    def scale(values, i):
        return jnp.concatenate(
            [values[:, c * third : (c + 1) * third] * factors[:, 4 * i + c : 4 * i + c + 1] for c in range(3)], axis=1
        ).astype(jnp.bfloat16)

    held_quarters = (t, across)

    def fill(a, i):
        q = held_quarters[i]
        cols = pl.ds(pl.multiple_of(q * quarter, 128), quarter)
        here = out_grad[:, cols] if a else scale(tokens[:, cols].astype(jnp.float32), i)
        outgoing[a, i] = message(picks[...], extra_picks[...], here).reshape(experts, 16, 4 * third)
        parts[a, q, me] = outgoing[a, i, me]

    def send(a, i, d):
        return pltpu.make_async_remote_copy(
            src_ref=outgoing.at[a, i, d], dst_ref=parts.at[a, held_quarters[i], me],
            send_sem=send_sem.at[a, i, d], recv_sem=recv_sem.at[a, i, me],
            device_id=(d, t), device_id_type=MESH,
        )

    def arrival(a, i, k):
        return pltpu.make_async_remote_copy(
            src_ref=outgoing.at[a, i, k], dst_ref=parts.at[a, held_quarters[i], k],
            send_sem=send_sem.at[a, i, k], recv_sem=recv_sem.at[a, i, k],
            device_id=(k, t), device_id_type=MESH,
        )

    groups = experts // 2

    def passing(a, kind, g):
        which, mate = ((t, buddy), (t, across), (across, buddy))[kind]
        block = parts.at[a, which, pl.ds(2 * g, 2)]
        return pltpu.make_async_remote_copy(
            src_ref=block, dst_ref=block,
            send_sem=pass_send.at[a, kind, g], recv_sem=pass_recv.at[a, kind, g],
            device_id=(me, mate), device_id_type=MESH,
        )

    def passed(a, kind, g):
        which, mate = ((buddy, buddy), (across, across), (diagonal, buddy))[kind]
        block = parts.at[a, which, pl.ds(2 * g, 2)]
        return pltpu.make_async_remote_copy(
            src_ref=block, dst_ref=block,
            send_sem=pass_send.at[a, kind, g], recv_sem=pass_recv.at[a, kind, g],
            device_id=(me, mate), device_id_type=MESH,
        )

    for a in range(2):
        loads[2 + a].wait()
        fill(a, 0)
        if a == 0:
            pl.semaphore_wait(barrier, len(peers) + len(mates))
        for d in peers:
            send(a, 0, d).start()
        fill(a, 1)
        for d in near:
            send(a, 1, d).start()
    for load in loads[5:]:
        load.start()

    my_slots = slots[pl.ds(me, 1), :] // tok_count
    owner_id = lax.broadcasted_iota(jnp.int32, (experts, capacity), 0)
    own_rank = ranks(jnp.broadcast_to(my_slots, (experts, capacity)) == owner_id)
    lead4 = 16.0 + lax.broadcasted_iota(jnp.int32, (4, capacity), 0).astype(jnp.float32)
    for k in range(experts):
        row_rank = own_rank[k : k + 1, :]
        place[pl.ds(k * 16, 16), :] = jnp.where(row_rank == lead_target, 1.0, 0.0)
        place[pl.ds(lead_rows + k * 4, 4), :] = jnp.where(row_rank == lead4, 1.0, 0.0)
    loads[4].wait()
    gate_flat = jnp.sum(place[...] * gates[...], axis=1, keepdims=True)

    rest_rows = experts * 4
    j = lax.broadcasted_iota(jnp.int32, (3 * rest_rows, lead_rows), 0)
    m = lax.broadcasted_iota(jnp.int32, (3 * rest_rows, lead_rows), 1)
    jr = j % rest_rows
    unpack = (m == (jr // 4) * 16 + 4 * (j // rest_rows) + jr % 4).astype(jnp.bfloat16)

    hidden_block = w_in.shape[1] // groups

    def block_of(i):
        return pl.ds(pl.multiple_of(i * hidden_block, hidden_block), hidden_block)

    near_first = [order[3], order[2], order[0], order[1]]

    def store(i):
        held, out = (
            (gate_held, gate_out), (token_held, token_out),
            (rows, rows_out), (hidden, hidden_out), (gated, gated_out), (dpre, dpre_out),
        )[i]
        return pltpu.make_async_copy(held, out, store_sem.at[i])

    def take_near(a):
        for i, kind in ((0, 0), (1, 2)):
            arrival(a, i, partner).wait_recv()
            passing(a, kind, order[3]).start()
            arrival(a, i, 2 * order[2]).wait_recv()
            arrival(a, i, 2 * order[2] + 1).wait_recv()
            passing(a, kind, order[2]).start()

    def take_far(a):
        for g in order[:2]:
            arrival(a, 0, 2 * g).wait_recv()
            arrival(a, 0, 2 * g + 1).wait_recv()
            passing(a, 1, g).start()
            passing(a, 0, g).start()

    def relay(a, g):
        passed(a, 1, g).wait_recv()
        passing(a, 2, g).start()

    def arrange(a, q, target):
        cols = pl.ds(pl.multiple_of(q * quarter, 128), quarter)
        target[pl.ds(0, lead_rows), cols] = parts[a, q, :, :, pl.ds(0, quarter)].reshape(lead_rows, quarter)
        rest = jnp.dot(
            unpack, parts[a, q, :, :, pl.ds(quarter, third)].reshape(lead_rows, third),
            preferred_element_type=jnp.float32,
        ).astype(jnp.bfloat16)
        for c in range(3):
            some = pl.ds(pl.multiple_of(q * quarter + c * third, 128), third)
            target[pl.ds(lead_rows, rest_rows), some] = rest[c * rest_rows : (c + 1) * rest_rows]
        return cols

    take_near(0)
    take_far(0)
    take_near(1)
    for g in order[:2]:
        relay(0, g)
    take_far(1)
    for kind in (0, 2):
        for g in near_first:
            passed(0, kind, g).wait_recv()
    for q in range(tensors):
        arrange(0, q, rows)
    loads[5].wait()
    for i in range(groups):
        cols = pl.ds(i * hidden_block, hidden_block)
        v = jnp.dot(rows[...], w_in[:, cols], preferred_element_type=jnp.float32)
        if i % 2 == 1:
            relay(1, order[i // 2])
        square = v * v
        tanh = jnp.tanh(ROOT * (v + CUBIC * v * square))
        half = 0.5 * (1.0 + tanh)
        hidden[:, cols] = (v * half).astype(jnp.bfloat16)
        slope[:, cols] = half + 0.5 * v * (1.0 - tanh * tanh) * (ROOT * (1.0 + 3.0 * CUBIC * square))

    store(2).start()
    store(3).start()

    loads[6].wait()
    for i, (q, kind) in enumerate(((t, None), (buddy, 0), (across, None))):
        if kind is not None:
            for g in near_first:
                passed(1, kind, g).wait_recv()
        part = arrange(1, q, grads)
        term = contract(grads[:, part], w_out[:, part], 1, 1)
        upstream[...] = term if i == 0 else upstream[...] + term
    for g in near_first:
        passed(1, 2, g).wait_recv()
    last_part = arrange(1, diagonal, grads)

    def backward(i, total):
        cols = block_of(i)
        up = upstream[:, cols] + contract(grads[:, last_part], w_out[cols, last_part], 1, 1)
        dpre[:, cols] = (gate_flat * up * slope[:, cols]).astype(jnp.bfloat16)
        return total + jnp.sum(hidden[:, cols].astype(jnp.float32) * up, axis=1, keepdims=True)

    gate_part = lax.fori_loop(0, groups, backward, jnp.zeros((place.shape[0], 1), jnp.float32))

    def slot_back(q):
        return contract(dpre[...], w_in[pl.ds(pl.multiple_of(q * quarter, 128), quarter), :], 1, 1)

    def to_core(i):
        return pltpu.make_async_remote_copy(
            src_ref=core_out.at[i], dst_ref=core_in.at[i], send_sem=ret_send.at[i], recv_sem=ret_recv.at[i],
            device_id=(me, buddy), device_id_type=MESH,
        )

    spans = [pl.ds(lead_rows, rest_rows)] + [pl.ds(pl.multiple_of(32 * g, 32), 32) for g in order]

    def to_side(i):
        return pltpu.make_async_remote_copy(
            src_ref=side_out.at[spans[i]], dst_ref=side_in.at[spans[i]],
            send_sem=side_send.at[i], recv_sem=side_recv.at[i],
            device_id=(me, across), device_id_type=MESH,
        )

    core_out[0] = slot_back(diagonal).astype(jnp.bfloat16)
    to_core(0).start()
    partial = slot_back(across)
    to_core(0).wait_recv()
    side_out[...] = (partial + core_in[0].astype(jnp.float32)).astype(jnp.bfloat16)
    for i in range(len(spans)):
        to_side(i).start()
    core_out[1] = slot_back(buddy).astype(jnp.bfloat16)
    to_core(1).start()
    mine[...] = slot_back(t)

    gate_parts[t] = jnp.broadcast_to(jnp.sum(place[...] * gate_part, axis=0, keepdims=True), (8, capacity))

    def gate_copy(i, slot):
        return pltpu.make_async_remote_copy(
            src_ref=gate_parts.at[t], dst_ref=gate_parts.at[slot], send_sem=gate_send.at[i], recv_sem=gate_recv.at[i],
            device_id=(me, mates[i]), device_id_type=MESH,
        )

    for i in range(3):
        gate_copy(i, t).start()

    gated[...] = (gate_flat * grads[...].astype(jnp.float32)).astype(jnp.bfloat16)
    to_core(1).wait_recv()
    mine[...] += core_in[1].astype(jnp.float32)

    def total(i):
        to_side(i).wait_recv()
        return (mine[spans[i], :] + side_in[spans[i], :].astype(jnp.float32)).astype(jnp.bfloat16)

    def give_back(d, slot):
        return pltpu.make_async_remote_copy(
            src_ref=back_out.at[d], dst_ref=back_in.at[slot], send_sem=back_send.at[d], recv_sem=back_recv.at[slot],
            device_id=(d, t), device_id_type=MESH,
        )

    tail = total(0)
    packed = sum(
        contract(unpack[c * rest_rows : (c + 1) * rest_rows], tail[:, c * third : (c + 1) * third], 0, 0)
        for c in range(3)
    ).astype(jnp.bfloat16)
    back_out[:, :, pl.ds(quarter, third)] = packed.reshape(experts, 16, third)
    for i, g in enumerate(order):
        back_out[pl.ds(2 * g, 2), :, pl.ds(0, quarter)] = total(i + 1).reshape(2, 16, quarter)
        if i < 3:
            give_back(2 * g, me).start()
            give_back(2 * g + 1, me).start()
        else:
            give_back(partner, me).start()
            back_in[me] = back_out[me]
    store(4).start()
    store(5).start()
    for a in range(2):
        for d in peers:
            send(a, 0, d).wait_send()
        for d in near:
            send(a, 1, d).wait_send()
        for g in order:
            passing(a, 0, g).wait_send()
            passing(a, 2, g).wait_send()
        for g in order[:2]:
            passing(a, 1, g).wait_send()
    for i in range(2):
        to_core(i).wait_send()
    for i in range(len(spans)):
        to_side(i).wait_send()
    for d in peers:
        give_back(d, d).wait_recv()
    sums = contract(picks[...], back_in[:, :, pl.ds(0, quarter)].reshape(lead_rows, quarter), 0, 0)
    returned = back_in[:, :, pl.ds(quarter, third)].reshape(lead_rows, third)
    pieces = [
        sums[:, c * third : (c + 1) * third] + contract(extra_picks[c], returned, 0, 0) for c in range(3)
    ]
    last_out[...] = scale(jnp.concatenate(pieces, axis=1), 0).reshape(tensors, tok_count // tensors, quarter)
    last_in[t] = last_out[t]

    def finish(i, slot):
        return pltpu.make_async_remote_copy(
            src_ref=last_out.at[mates[i]], dst_ref=last_in.at[slot], send_sem=last_send.at[i], recv_sem=last_recv.at[i],
            device_id=(me, mates[i]), device_id_type=MESH,
        )

    for i in range(3):
        finish(i, t).start()
    for i in range(3):
        gate_copy(i, mates[i]).wait_recv()
    gate_held[...] = (gate_parts[0] + gate_parts[1] + gate_parts[2] + gate_parts[3])[0:1]
    store(0).start()
    for i in range(3):
        finish(i, mates[i]).wait_recv()
    for q in range(tensors):
        token_held[:, pl.ds(q * quarter, quarter)] = last_in[q]
    store(1).start()

    for d in peers:
        give_back(d, me).wait_send()
    for i in range(3):
        gate_copy(i, t).wait_send()
        finish(i, t).wait_send()
    for i in range(6):
        store(i).wait()


def exchange(experts, tensors, tokens, exponents, out_grad, slots, gates, w_in, w_out):
    tok_count, width = tokens.shape
    hid = w_in.shape[1]
    quarter = width // tensors
    wide = quarter + quarter // 3
    count = experts * 20
    bf16, f32 = jnp.bfloat16, jnp.float32
    hbm = pl.BlockSpec(memory_space=pltpu.HBM)
    dma = pltpu.SemaphoreType.DMA
    return pl.pallas_call(
        functools.partial(exchange_kernel, experts, tensors),
        out_shape=(
            jax.ShapeDtypeStruct((tok_count // tensors, width), bf16),
            jax.ShapeDtypeStruct(gates.shape, f32),
            jax.ShapeDtypeStruct((count, width), bf16),
            jax.ShapeDtypeStruct((count, width), bf16),
            jax.ShapeDtypeStruct((count, hid), bf16),
            jax.ShapeDtypeStruct((count, hid), bf16),
        ),
        in_specs=[hbm] * 7,
        out_specs=(hbm,) * 6,
        scratch_shapes=[
            pltpu.VMEM((tok_count // tensors, width), bf16),
            pltpu.VMEM(gates.shape, f32),
            pltpu.VMEM((count, width), bf16),
            pltpu.VMEM((count, width), bf16),
            pltpu.VMEM((count, hid), bf16),
            pltpu.VMEM((count, hid), bf16),
            pltpu.VMEM(tokens.shape, bf16),
            pltpu.VMEM(exponents.shape, jnp.int32),
            pltpu.VMEM(out_grad.shape, bf16),
            pltpu.VMEM(slots.shape, jnp.int32),
            pltpu.VMEM(gates.shape, f32),
            pltpu.VMEM(w_in.shape, bf16),
            pltpu.VMEM(w_out.shape, bf16),
            pltpu.VMEM((experts * 16, tok_count), bf16),
            pltpu.VMEM((3, experts * 16, tok_count), bf16),
            pltpu.VMEM((count, slots.shape[1]), f32),
            pltpu.VMEM((2, 2, experts, 16, wide), bf16),
            pltpu.VMEM((2, tensors, experts, 16, wide), bf16),
            pltpu.VMEM((count, width), bf16),
            pltpu.VMEM((count, hid), f32),
            pltpu.VMEM((count, hid), f32),
            pltpu.VMEM((2, count, quarter), bf16),
            pltpu.VMEM((2, count, quarter), bf16),
            pltpu.VMEM((count, quarter), bf16),
            pltpu.VMEM((count, quarter), bf16),
            pltpu.VMEM((count, quarter), f32),
            pltpu.VMEM((experts, 16, wide), bf16),
            pltpu.VMEM((experts, 16, wide), bf16),
            pltpu.VMEM((tensors, tok_count // tensors, quarter), bf16),
            pltpu.VMEM((tensors, tok_count // tensors, quarter), bf16),
            pltpu.VMEM((tensors, 8, slots.shape[1]), f32),
            dma((7,)),
            dma((2, 2, experts)),
            dma((2, 2, experts)),
            dma((2, 3, experts // 2)),
            dma((2, 3, experts // 2)),
            dma((2,)),
            dma((2,)),
            dma((5,)),
            dma((5,)),
            dma((experts,)),
            dma((experts,)),
            dma((3,)),
            dma((3,)),
            dma((3,)),
            dma((3,)),
            dma((6,)),
        ],
        compiler_params=pltpu.CompilerParams(
            collective_id=0, has_side_effects=True, vmem_limit_bytes=60 * 2**20
        ),
    )(tokens, exponents, out_grad, slots, gates, w_in, w_out)


def weights_kernel(
    token_hbm, gate_hbm, rows_hbm, gated_hbm, hidden_hbm, dpre_hbm,
    token_out, gate_out, in_out, out_out,
    rows, gated, hidden, dpre, token_held, gate_held, in_held, out_held, load_sem, sem,
):
    sources = (hidden_hbm, gated_hbm, rows_hbm, dpre_hbm, token_hbm, gate_hbm)
    helds = (hidden, gated, rows, dpre, token_held, gate_held)
    loads = [
        pltpu.make_async_copy(source, held, load_sem.at[i]) for i, (source, held) in enumerate(zip(sources, helds))
    ]
    for load in loads:
        load.start()
    chunks = 4
    copies = []
    for n, (left, right, held, out) in enumerate(((hidden, gated, out_held, out_out), (rows, dpre, in_held, in_out))):
        loads[2 * n].wait()
        loads[2 * n + 1].wait()
        for i in range(chunks):
            size = out.shape[0] // chunks
            span = pl.ds(i * size, size)
            held[span, :] = contract(left[:, span], right[...], 0, 0).astype(jnp.bfloat16)
            copies.append(pltpu.make_async_copy(held.at[span], out.at[span], sem.at[len(copies)]))
            copies[-1].start()
        if n == 0:
            for i, (held, out) in enumerate(((token_held, token_out), (gate_held, gate_out))):
                loads[4 + i].wait()
                copies.append(pltpu.make_async_copy(held, out, sem.at[len(copies)]))
                copies[-1].start()
    for copy in copies:
        copy.wait()


def weight_grads(token_grad, gate_grad, rows, gated, hidden, dpre):
    width, hid = rows.shape[1], hidden.shape[1]
    bf16 = jnp.bfloat16
    like = lambda array: jax.ShapeDtypeStruct(array.shape, array.dtype)
    hbm = pl.BlockSpec(memory_space=pltpu.HBM)
    return pl.pallas_call(
        weights_kernel,
        out_shape=(
            like(token_grad), like(gate_grad),
            jax.ShapeDtypeStruct((width, hid), bf16), jax.ShapeDtypeStruct((hid, width), bf16),
        ),
        in_specs=[hbm] * 6,
        out_specs=(hbm,) * 4,
        scratch_shapes=[
            pltpu.VMEM(array.shape, array.dtype) for array in (rows, gated, hidden, dpre, token_grad, gate_grad)
        ]
        + [
            pltpu.VMEM((width, hid), bf16),
            pltpu.VMEM((hid, width), bf16),
            pltpu.SemaphoreType.DMA((6,)),
            pltpu.SemaphoreType.DMA((10,)),
        ],
        compiler_params=pltpu.CompilerParams(vmem_limit_bytes=60 * 2**20),
    )(token_grad, gate_grad, rows, gated, hidden, dpre)


def local_fused(tokens, exponents, out_grad, slots, gates, w_in, w_out):
    results = exchange(
        lax.axis_size("expert"), lax.axis_size("tensor"),
        tokens, exponents.T, out_grad, slots, gates, w_in[0], w_out[0],
    )
    token_grad, gate_grad, in_weight_grad, out_weight_grad = weight_grads(*results)
    return (token_grad, in_weight_grad[None], out_weight_grad[None], gate_grad)


def fits_exchange(mesh):
    return mesh.shape["expert"] == 8 and mesh.shape["tensor"] == 4


def solution(mesh):
    placed = (
        P("expert", None),
        P("expert", None),
        P("expert", None),
        P(),
        P("expert", None),
        P("expert", None, "tensor"),
        P("expert", "tensor", None),
    )
    return jax.shard_map(
        local_fused if fits_exchange(mesh) else local,
        mesh=mesh,
        in_specs=placed,
        out_specs=(
            P(("expert", "tensor"), None),
            P("expert", None, "tensor"),
            P("expert", "tensor", None),
            P("expert", None),
        ),
        check_vma=False,
    )
```

```python
import functools
import math

import jax
import jax.numpy as jnp
from jax import lax
from jax.experimental import pallas as pl
from jax.experimental.pallas import tpu as pltpu
from jax.sharding import PartitionSpec as P

MESH = pl.DeviceIdType.MESH
ROOT = math.sqrt(2.0 / math.pi)
CUBIC = 0.044715


def contract(left, right, left_dim, right_dim):
    return lax.dot_general(
        left, right, (((left_dim,), (right_dim,)), ((), ())), preferred_element_type=jnp.float32
    )


def apply_scales(values, exponents):
    row_count = values.shape[0]
    block_count = exponents.shape[1]
    factors = jnp.exp2(exponents.astype(jnp.float32))
    widened = values.astype(jnp.float32).reshape(row_count, block_count, 128) * factors[:, :, None]
    return widened.reshape(row_count, block_count * 128)


def local(tokens, exponents, out_grad, slots, gates, w_in, w_out):
    expert_count = lax.axis_size("expert")
    my_expert = lax.axis_index("expert")
    my_tensor = lax.axis_index("tensor")
    tok_count = tokens.shape[0]
    model_width = tokens.shape[1]
    slot_count = slots.shape[1]
    capacity = slot_count // expert_count + slot_count // (4 * expert_count)
    total_slots = expert_count * capacity
    owner = slots // tok_count
    local_index = slots % tok_count
    from_here = owner == my_expert
    send_order = jnp.cumsum(from_here.astype(jnp.int32), axis=1) - 1
    rank_range = jnp.arange(capacity, dtype=jnp.int32)
    send_hit = from_here[:, :, None] & (send_order[:, :, None] == rank_range[None, None, :])
    send_valid = jnp.any(send_hit, axis=1)
    picked_index = jnp.sum(jnp.where(send_hit, local_index[:, :, None], 0), axis=1)
    send_table = jnp.where(send_valid, picked_index, tok_count)
    row_owner = lax.dynamic_index_in_dim(owner, my_expert, 0, keepdims=False)
    slot_range = jnp.arange(slot_count, dtype=jnp.int32)
    earlier = (row_owner[:, None] == row_owner[None, :]) & (
        slot_range[:, None] > slot_range[None, :]
    )
    row_rank = jnp.sum(earlier.astype(jnp.int32), axis=1)
    flat_index = row_owner * capacity + row_rank
    scaled_local = apply_scales(tokens, exponents).astype(jnp.bfloat16)
    sent_rows = jnp.take(scaled_local, send_table, axis=0, mode="fill", fill_value=0)
    sent_grads = jnp.take(out_grad, send_table, axis=0, mode="fill", fill_value=0)
    arrived_rows, arrived_grads = (
        lax.all_to_all(sent_rows, "expert", split_axis=0, concat_axis=0, tiled=True),
        lax.all_to_all(sent_grads, "expert", split_axis=0, concat_axis=0, tiled=True),
    )
    slot_rows = arrived_rows.reshape(total_slots, model_width)
    slot_grads = arrived_grads.reshape(total_slots, model_width)
    gate_row = jnp.zeros((total_slots,), jnp.float32).at[flat_index].set(gates[0])
    weight_in = w_in[0]
    weight_out = w_out[0]
    preact = jnp.dot(slot_rows, weight_in, preferred_element_type=jnp.float32)
    hidden_full, backward = jax.vjp(jax.nn.gelu, preact)
    hidden = hidden_full.astype(jnp.bfloat16)
    upstream = contract(slot_grads, weight_out, 1, 1)
    gate_part = jnp.sum(hidden.astype(jnp.float32) * upstream, axis=1)
    gate_total = lax.psum(gate_part[flat_index], "tensor")
    dpre = backward(gate_row[:, None] * upstream)[0].astype(jnp.bfloat16)
    gated_grads = (gate_row[:, None] * slot_grads.astype(jnp.float32)).astype(jnp.bfloat16)
    out_weight_grad = contract(hidden, gated_grads, 0, 0).astype(jnp.bfloat16)
    in_weight_grad = contract(slot_rows, dpre, 0, 0).astype(jnp.bfloat16)
    slot_back = contract(dpre, weight_in, 1, 1)
    flat_send = send_table.reshape(-1)
    came_back = lax.all_to_all(
        slot_back.reshape(expert_count, capacity, model_width),
        "expert",
        split_axis=0,
        concat_axis=0,
        tiled=True,
    )
    token_sums = (
        jnp.zeros((tok_count, model_width), jnp.float32)
        .at[flat_send]
        .add(came_back.reshape(total_slots, model_width), mode="drop")
    )
    my_share = lax.psum_scatter(token_sums, "tensor", scatter_dimension=0, tiled=True)
    share_rows = my_share.shape[0]
    my_scales = lax.dynamic_slice_in_dim(exponents, my_tensor * share_rows, share_rows, 0)
    token_grad = apply_scales(my_share, my_scales).astype(jnp.bfloat16)
    return (token_grad, in_weight_grad[None], out_weight_grad[None], gate_total[None])


def message(picks, extra_picks, rows):
    third = rows.shape[1] // 3
    lead = jnp.dot(picks, rows, preferred_element_type=jnp.float32)
    rest = sum(
        jnp.dot(extra_picks[c], rows[:, c * third : (c + 1) * third], preferred_element_type=jnp.float32)
        for c in range(3)
    )
    return jnp.concatenate([lead, rest], axis=1).astype(jnp.bfloat16)


def exchange_kernel(
    experts, tensors,
    tokens_hbm, exponents_hbm, out_grad_hbm, slots_hbm, gates_hbm, w_in_hbm, w_out_hbm,
    token_out, gate_out, rows_out, gated_out, hidden_out, dpre_out,
    token_held, gate_held, rows, gated, hidden, dpre,
    tokens, exponents, out_grad, slots, gates,
    w_in, w_out, picks, extra_picks, place, outgoing, parts, grads, slope,
    core_out, core_in, side_out, side_in, mine, back_out, back_in, last_out, last_in, gate_parts,
    load_sem, send_sem, recv_sem, pass_send, pass_recv, ret_send, ret_recv, side_send, side_recv,
    back_send, back_recv, last_send, last_recv, gate_send, gate_recv, store_sem,
):
    me = lax.axis_index("expert")
    t = lax.axis_index("tensor")
    y, core = t // 2, t % 2
    buddy = 2 * y + (1 - core)
    across = 2 * (1 - y) + core
    diagonal = 2 * (1 - y) + (1 - core)
    tok_count, width = tokens.shape
    quarter = width // tensors
    third = quarter // 3
    capacity = slots.shape[1]
    lead_rows = experts * 16

    loads = [
        pltpu.make_async_copy(source, held, load_sem.at[i])
        for i, (source, held) in enumerate(
            (
                (slots_hbm, slots), (exponents_hbm, exponents), (tokens_hbm, tokens), (out_grad_hbm, out_grad),
                (gates_hbm, gates), (w_in_hbm, w_in), (w_out_hbm, w_out),
            )
        )
    ]
    for load in loads[:5]:
        load.start()

    barrier = pltpu.get_barrier_semaphore()
    z, x = me // 2, me % 2
    order = [(z + 2) % 4, 3 - z, z + 1 - 2 * (z % 2), z]
    partner = 2 * z + 1 - x
    peers = [2 * g + i for g in order[:3] for i in (x, 1 - x)] + [partner]
    mates = [buddy, across, diagonal]
    for d in peers:
        pl.semaphore_signal(barrier, inc=1, device_id=(d, t), device_id_type=MESH)
    for m in mates:
        pl.semaphore_signal(barrier, inc=1, device_id=(me, m), device_id_type=MESH)

    tri = (
        lax.broadcasted_iota(jnp.int32, (capacity, capacity), 0)
        < lax.broadcasted_iota(jnp.int32, (capacity, capacity), 1)
    ).astype(jnp.bfloat16)

    def ranks(mask):
        ones = jnp.where(mask, 1.0, 0.0)
        before = jnp.dot(ones.astype(jnp.bfloat16), tri, preferred_element_type=jnp.float32)
        return jnp.where(mask, before, -1.0)

    loads[0].wait()
    all_slots = slots[...]
    local_index = all_slots - me * tok_count
    rank = ranks((local_index >= 0) & (local_index < tok_count))
    local_number = local_index.astype(jnp.float32) + 1.0
    row_id = lax.broadcasted_iota(jnp.int32, (16, capacity), 0)
    lead_target = row_id.astype(jnp.float32)
    rest_target = (16 + row_id % 4).astype(jnp.float32)
    token_id = lax.broadcasted_iota(jnp.int32, (16, tok_count), 1).astype(jnp.float32) + 1.0
    part_id = lax.broadcasted_iota(jnp.int32, (16, tok_count), 0) // 4
    for d in range(experts):
        row_rank, row_number = rank[d : d + 1, :], local_number[d : d + 1, :]
        lead = jnp.sum(jnp.where(row_rank == lead_target, row_number, 0.0), axis=1, keepdims=True)
        rest = jnp.sum(jnp.where(row_rank == rest_target, row_number, 0.0), axis=1, keepdims=True)
        span = pl.ds(d * 16, 16)
        picks[span, :] = jnp.where(lead == token_id, 1.0, 0.0).astype(jnp.bfloat16)
        rest_hit = jnp.where(rest == token_id, 1.0, 0.0)
        for c in range(3):
            extra_picks[c, span, :] = jnp.where(part_id == c, rest_hit, 0.0).astype(jnp.bfloat16)

    blocks = exponents.shape[0]
    chosen = (
        lax.broadcasted_iota(jnp.int32, (blocks, 4), 0) == 3 * t + lax.broadcasted_iota(jnp.int32, (blocks, 4), 1)
    ).astype(jnp.bfloat16)
    loads[1].wait()
    factors = contract(jnp.exp2(exponents[...].astype(jnp.float32)).astype(jnp.bfloat16), chosen, 0, 0)
    my_cols = pl.ds(pl.multiple_of(t * quarter, 128), quarter)

    def scale(values):
        return jnp.concatenate(
            [values[:, c * third : (c + 1) * third] * factors[:, c : c + 1] for c in range(3)], axis=1
        ).astype(jnp.bfloat16)

    def fill(a, mine_here):
        outgoing[a] = message(picks[...], extra_picks[...], mine_here).reshape(experts, 16, 4 * third)
        parts[a, t, me] = outgoing[a, me]

    def send(a, d):
        return pltpu.make_async_remote_copy(
            src_ref=outgoing.at[a, d], dst_ref=parts.at[a, t, me],
            send_sem=send_sem.at[a, d], recv_sem=recv_sem.at[a, me],
            device_id=(d, t), device_id_type=MESH,
        )

    def arrival(a, k):
        return pltpu.make_async_remote_copy(
            src_ref=outgoing.at[a, k], dst_ref=parts.at[a, t, k],
            send_sem=send_sem.at[a, k], recv_sem=recv_sem.at[a, k],
            device_id=(k, t), device_id_type=MESH,
        )

    groups = experts // 2

    def passing(a, kind, g):
        which, mate = ((t, buddy), (t, across), (across, buddy))[kind]
        block = parts.at[a, which, pl.ds(2 * g, 2)]
        return pltpu.make_async_remote_copy(
            src_ref=block, dst_ref=block,
            send_sem=pass_send.at[a, kind, g], recv_sem=pass_recv.at[a, kind, g],
            device_id=(me, mate), device_id_type=MESH,
        )

    def passed(a, kind, g):
        which, mate = ((buddy, buddy), (across, across), (diagonal, buddy))[kind]
        block = parts.at[a, which, pl.ds(2 * g, 2)]
        return pltpu.make_async_remote_copy(
            src_ref=block, dst_ref=block,
            send_sem=pass_send.at[a, kind, g], recv_sem=pass_recv.at[a, kind, g],
            device_id=(me, mate), device_id_type=MESH,
        )

    loads[2].wait()
    fill(0, scale(tokens[:, my_cols].astype(jnp.float32)))
    pl.semaphore_wait(barrier, len(peers) + len(mates))
    for d in peers:
        send(0, d).start()
    loads[3].wait()
    fill(1, out_grad[:, my_cols])
    for d in peers:
        send(1, d).start()
    for load in loads[5:]:
        load.start()

    my_slots = slots[pl.ds(me, 1), :] // tok_count
    owner_id = lax.broadcasted_iota(jnp.int32, (experts, capacity), 0)
    own_rank = ranks(jnp.broadcast_to(my_slots, (experts, capacity)) == owner_id)
    lead4 = 16.0 + lax.broadcasted_iota(jnp.int32, (4, capacity), 0).astype(jnp.float32)
    for k in range(experts):
        row_rank = own_rank[k : k + 1, :]
        place[pl.ds(k * 16, 16), :] = jnp.where(row_rank == lead_target, 1.0, 0.0)
        place[pl.ds(lead_rows + k * 4, 4), :] = jnp.where(row_rank == lead4, 1.0, 0.0)
    loads[4].wait()
    gate_flat = jnp.sum(place[...] * gates[...], axis=1, keepdims=True)

    rest_rows = experts * 4
    j = lax.broadcasted_iota(jnp.int32, (3 * rest_rows, lead_rows), 0)
    m = lax.broadcasted_iota(jnp.int32, (3 * rest_rows, lead_rows), 1)
    jr = j % rest_rows
    unpack = (m == (jr // 4) * 16 + 4 * (j // rest_rows) + jr % 4).astype(jnp.bfloat16)

    hidden_block = w_in.shape[1] // groups

    def block_of(i):
        return pl.ds(pl.multiple_of(i * hidden_block, hidden_block), hidden_block)

    near_first = [order[3], order[2], order[0], order[1]]

    def store(i):
        held, out = (
            (gate_held, gate_out), (token_held, token_out),
            (rows, rows_out), (hidden, hidden_out), (gated, gated_out), (dpre, dpre_out),
        )[i]
        return pltpu.make_async_copy(held, out, store_sem.at[i])

    def take(a, g):
        if g is order[3]:
            arrival(a, partner).wait_recv()
        else:
            arrival(a, 2 * g).wait_recv()
            arrival(a, 2 * g + 1).wait_recv()
        passing(a, 1, g).start()
        passing(a, 0, g).start()

    def relay(a, g):
        passed(a, 1, g).wait_recv()
        passing(a, 2, g).start()

    def arrange(a, q, target):
        cols = pl.ds(pl.multiple_of(q * quarter, 128), quarter)
        target[pl.ds(0, lead_rows), cols] = parts[a, q, :, :, pl.ds(0, quarter)].reshape(lead_rows, quarter)
        rest = jnp.dot(
            unpack, parts[a, q, :, :, pl.ds(quarter, third)].reshape(lead_rows, third),
            preferred_element_type=jnp.float32,
        ).astype(jnp.bfloat16)
        for c in range(3):
            some = pl.ds(pl.multiple_of(q * quarter + c * third, 128), third)
            target[pl.ds(lead_rows, rest_rows), some] = rest[c * rest_rows : (c + 1) * rest_rows]
        return cols

    for a in range(2):
        for g in near_first:
            take(a, g)
    for g in near_first:
        relay(0, g)
    for kind in (0, 2):
        for g in near_first:
            passed(0, kind, g).wait_recv()
    for q in range(tensors):
        arrange(0, q, rows)
    loads[5].wait()
    for i, g in enumerate(near_first):
        cols = pl.ds(i * hidden_block, hidden_block)
        v = jnp.dot(rows[...], w_in[:, cols], preferred_element_type=jnp.float32)
        relay(1, g)
        square = v * v
        tanh = jnp.tanh(ROOT * (v + CUBIC * v * square))
        half = 0.5 * (1.0 + tanh)
        hidden[:, cols] = (v * half).astype(jnp.bfloat16)
        slope[:, cols] = half + 0.5 * v * (1.0 - tanh * tanh) * (ROOT * (1.0 + 3.0 * CUBIC * square))

    store(2).start()
    store(3).start()

    loads[6].wait()
    for kind in (0, 2):
        for g in near_first:
            passed(1, kind, g).wait_recv()
    for q in range(tensors):
        arrange(1, q, grads)

    def backward(i, total):
        cols = block_of(i)
        up = contract(grads[...], w_out[cols, :], 1, 1)
        dpre[:, cols] = (gate_flat * up * slope[:, cols]).astype(jnp.bfloat16)
        return total + jnp.sum(hidden[:, cols].astype(jnp.float32) * up, axis=1, keepdims=True)

    gate_part = lax.fori_loop(0, groups, backward, jnp.zeros((place.shape[0], 1), jnp.float32))

    def slot_back(q):
        return contract(dpre[...], w_in[pl.ds(pl.multiple_of(q * quarter, 128), quarter), :], 1, 1)

    def to_core(i):
        return pltpu.make_async_remote_copy(
            src_ref=core_out.at[i], dst_ref=core_in.at[i], send_sem=ret_send.at[i], recv_sem=ret_recv.at[i],
            device_id=(me, buddy), device_id_type=MESH,
        )

    spans = [pl.ds(lead_rows, rest_rows)] + [pl.ds(pl.multiple_of(32 * g, 32), 32) for g in order]

    def to_side(i):
        return pltpu.make_async_remote_copy(
            src_ref=side_out.at[spans[i]], dst_ref=side_in.at[spans[i]],
            send_sem=side_send.at[i], recv_sem=side_recv.at[i],
            device_id=(me, across), device_id_type=MESH,
        )

    core_out[0] = slot_back(diagonal).astype(jnp.bfloat16)
    to_core(0).start()
    partial = slot_back(across)
    to_core(0).wait_recv()
    side_out[...] = (partial + core_in[0].astype(jnp.float32)).astype(jnp.bfloat16)
    for i in range(len(spans)):
        to_side(i).start()
    core_out[1] = slot_back(buddy).astype(jnp.bfloat16)
    to_core(1).start()
    mine[...] = slot_back(t)

    gate_parts[t] = jnp.broadcast_to(jnp.sum(place[...] * gate_part, axis=0, keepdims=True), (8, capacity))

    def gate_copy(i, slot):
        return pltpu.make_async_remote_copy(
            src_ref=gate_parts.at[t], dst_ref=gate_parts.at[slot], send_sem=gate_send.at[i], recv_sem=gate_recv.at[i],
            device_id=(me, mates[i]), device_id_type=MESH,
        )

    for i in range(3):
        gate_copy(i, t).start()

    gated[...] = (gate_flat * grads[...].astype(jnp.float32)).astype(jnp.bfloat16)
    to_core(1).wait_recv()
    mine[...] += core_in[1].astype(jnp.float32)

    def total(i):
        to_side(i).wait_recv()
        return (mine[spans[i], :] + side_in[spans[i], :].astype(jnp.float32)).astype(jnp.bfloat16)

    def give_back(d, slot):
        return pltpu.make_async_remote_copy(
            src_ref=back_out.at[d], dst_ref=back_in.at[slot], send_sem=back_send.at[d], recv_sem=back_recv.at[slot],
            device_id=(d, t), device_id_type=MESH,
        )

    tail = total(0)
    packed = sum(
        contract(unpack[c * rest_rows : (c + 1) * rest_rows], tail[:, c * third : (c + 1) * third], 0, 0)
        for c in range(3)
    ).astype(jnp.bfloat16)
    back_out[:, :, pl.ds(quarter, third)] = packed.reshape(experts, 16, third)
    for i, g in enumerate(order):
        back_out[pl.ds(2 * g, 2), :, pl.ds(0, quarter)] = total(i + 1).reshape(2, 16, quarter)
        if i < 3:
            give_back(2 * g, me).start()
            give_back(2 * g + 1, me).start()
        else:
            give_back(partner, me).start()
            back_in[me] = back_out[me]
    store(4).start()
    store(5).start()
    for a in range(2):
        for d in peers:
            send(a, d).wait_send()
        for kind in range(3):
            for g in range(groups):
                passing(a, kind, g).wait_send()
    for i in range(2):
        to_core(i).wait_send()
    for i in range(len(spans)):
        to_side(i).wait_send()
    for d in peers:
        give_back(d, d).wait_recv()
    sums = contract(picks[...], back_in[:, :, pl.ds(0, quarter)].reshape(lead_rows, quarter), 0, 0)
    returned = back_in[:, :, pl.ds(quarter, third)].reshape(lead_rows, third)
    pieces = [
        sums[:, c * third : (c + 1) * third] + contract(extra_picks[c], returned, 0, 0) for c in range(3)
    ]
    last_out[...] = scale(jnp.concatenate(pieces, axis=1)).reshape(tensors, tok_count // tensors, quarter)
    last_in[t] = last_out[t]

    def finish(i, slot):
        return pltpu.make_async_remote_copy(
            src_ref=last_out.at[mates[i]], dst_ref=last_in.at[slot], send_sem=last_send.at[i], recv_sem=last_recv.at[i],
            device_id=(me, mates[i]), device_id_type=MESH,
        )

    for i in range(3):
        finish(i, t).start()
    for i in range(3):
        gate_copy(i, mates[i]).wait_recv()
    gate_held[...] = (gate_parts[0] + gate_parts[1] + gate_parts[2] + gate_parts[3])[0:1]
    store(0).start()
    for i in range(3):
        finish(i, mates[i]).wait_recv()
    for q in range(tensors):
        token_held[:, pl.ds(q * quarter, quarter)] = last_in[q]
    store(1).start()

    for d in peers:
        give_back(d, me).wait_send()
    for i in range(3):
        gate_copy(i, t).wait_send()
        finish(i, t).wait_send()
    for i in range(6):
        store(i).wait()


def exchange(experts, tensors, tokens, exponents, out_grad, slots, gates, w_in, w_out):
    tok_count, width = tokens.shape
    hid = w_in.shape[1]
    quarter = width // tensors
    wide = quarter + quarter // 3
    count = experts * 20
    bf16, f32 = jnp.bfloat16, jnp.float32
    hbm = pl.BlockSpec(memory_space=pltpu.HBM)
    dma = pltpu.SemaphoreType.DMA
    return pl.pallas_call(
        functools.partial(exchange_kernel, experts, tensors),
        out_shape=(
            jax.ShapeDtypeStruct((tok_count // tensors, width), bf16),
            jax.ShapeDtypeStruct(gates.shape, f32),
            jax.ShapeDtypeStruct((count, width), bf16),
            jax.ShapeDtypeStruct((count, width), bf16),
            jax.ShapeDtypeStruct((count, hid), bf16),
            jax.ShapeDtypeStruct((count, hid), bf16),
        ),
        in_specs=[hbm] * 7,
        out_specs=(hbm,) * 6,
        scratch_shapes=[
            pltpu.VMEM((tok_count // tensors, width), bf16),
            pltpu.VMEM(gates.shape, f32),
            pltpu.VMEM((count, width), bf16),
            pltpu.VMEM((count, width), bf16),
            pltpu.VMEM((count, hid), bf16),
            pltpu.VMEM((count, hid), bf16),
            pltpu.VMEM(tokens.shape, bf16),
            pltpu.VMEM(exponents.shape, jnp.int32),
            pltpu.VMEM(out_grad.shape, bf16),
            pltpu.VMEM(slots.shape, jnp.int32),
            pltpu.VMEM(gates.shape, f32),
            pltpu.VMEM(w_in.shape, bf16),
            pltpu.VMEM(w_out.shape, bf16),
            pltpu.VMEM((experts * 16, tok_count), bf16),
            pltpu.VMEM((3, experts * 16, tok_count), bf16),
            pltpu.VMEM((count, slots.shape[1]), f32),
            pltpu.VMEM((2, experts, 16, wide), bf16),
            pltpu.VMEM((2, tensors, experts, 16, wide), bf16),
            pltpu.VMEM((count, width), bf16),
            pltpu.VMEM((count, hid), f32),
            pltpu.VMEM((2, count, quarter), bf16),
            pltpu.VMEM((2, count, quarter), bf16),
            pltpu.VMEM((count, quarter), bf16),
            pltpu.VMEM((count, quarter), bf16),
            pltpu.VMEM((count, quarter), f32),
            pltpu.VMEM((experts, 16, wide), bf16),
            pltpu.VMEM((experts, 16, wide), bf16),
            pltpu.VMEM((tensors, tok_count // tensors, quarter), bf16),
            pltpu.VMEM((tensors, tok_count // tensors, quarter), bf16),
            pltpu.VMEM((tensors, 8, slots.shape[1]), f32),
            dma((7,)),
            dma((2, experts)),
            dma((2, experts)),
            dma((2, 3, experts // 2)),
            dma((2, 3, experts // 2)),
            dma((2,)),
            dma((2,)),
            dma((5,)),
            dma((5,)),
            dma((experts,)),
            dma((experts,)),
            dma((3,)),
            dma((3,)),
            dma((3,)),
            dma((3,)),
            dma((6,)),
        ],
        compiler_params=pltpu.CompilerParams(
            collective_id=0, has_side_effects=True, vmem_limit_bytes=60 * 2**20
        ),
    )(tokens, exponents, out_grad, slots, gates, w_in, w_out)


def weights_kernel(
    token_hbm, gate_hbm, rows_hbm, gated_hbm, hidden_hbm, dpre_hbm,
    token_out, gate_out, in_out, out_out,
    rows, gated, hidden, dpre, token_held, gate_held, in_held, out_held, load_sem, sem,
):
    sources = (hidden_hbm, gated_hbm, rows_hbm, dpre_hbm, token_hbm, gate_hbm)
    helds = (hidden, gated, rows, dpre, token_held, gate_held)
    loads = [
        pltpu.make_async_copy(source, held, load_sem.at[i]) for i, (source, held) in enumerate(zip(sources, helds))
    ]
    for load in loads:
        load.start()
    chunks = 4
    copies = []
    for n, (left, right, held, out) in enumerate(((hidden, gated, out_held, out_out), (rows, dpre, in_held, in_out))):
        loads[2 * n].wait()
        loads[2 * n + 1].wait()
        for i in range(chunks):
            size = out.shape[0] // chunks
            span = pl.ds(i * size, size)
            held[span, :] = contract(left[:, span], right[...], 0, 0).astype(jnp.bfloat16)
            copies.append(pltpu.make_async_copy(held.at[span], out.at[span], sem.at[len(copies)]))
            copies[-1].start()
        if n == 0:
            for i, (held, out) in enumerate(((token_held, token_out), (gate_held, gate_out))):
                loads[4 + i].wait()
                copies.append(pltpu.make_async_copy(held, out, sem.at[len(copies)]))
                copies[-1].start()
    for copy in copies:
        copy.wait()


def weight_grads(token_grad, gate_grad, rows, gated, hidden, dpre):
    width, hid = rows.shape[1], hidden.shape[1]
    bf16 = jnp.bfloat16
    like = lambda array: jax.ShapeDtypeStruct(array.shape, array.dtype)
    hbm = pl.BlockSpec(memory_space=pltpu.HBM)
    return pl.pallas_call(
        weights_kernel,
        out_shape=(
            like(token_grad), like(gate_grad),
            jax.ShapeDtypeStruct((width, hid), bf16), jax.ShapeDtypeStruct((hid, width), bf16),
        ),
        in_specs=[hbm] * 6,
        out_specs=(hbm,) * 4,
        scratch_shapes=[
            pltpu.VMEM(array.shape, array.dtype) for array in (rows, gated, hidden, dpre, token_grad, gate_grad)
        ]
        + [
            pltpu.VMEM((width, hid), bf16),
            pltpu.VMEM((hid, width), bf16),
            pltpu.SemaphoreType.DMA((6,)),
            pltpu.SemaphoreType.DMA((10,)),
        ],
        compiler_params=pltpu.CompilerParams(vmem_limit_bytes=60 * 2**20),
    )(token_grad, gate_grad, rows, gated, hidden, dpre)


def local_fused(tokens, exponents, out_grad, slots, gates, w_in, w_out):
    results = exchange(
        lax.axis_size("expert"), lax.axis_size("tensor"),
        tokens, exponents.T, out_grad, slots, gates, w_in[0], w_out[0],
    )
    token_grad, gate_grad, in_weight_grad, out_weight_grad = weight_grads(*results)
    return (token_grad, in_weight_grad[None], out_weight_grad[None], gate_grad)


def fits_exchange(mesh):
    return mesh.shape["expert"] == 8 and mesh.shape["tensor"] == 4


def solution(mesh):
    placed = (
        P("expert", None),
        P("expert", None),
        P("expert", None),
        P(),
        P("expert", None),
        P("expert", None, "tensor"),
        P("expert", "tensor", None),
    )
    return jax.shard_map(
        local_fused if fits_exchange(mesh) else local,
        mesh=mesh,
        in_specs=placed,
        out_specs=(
            P(("expert", "tensor"), None),
            P("expert", None, "tensor"),
            P("expert", "tensor", None),
            P("expert", None),
        ),
        check_vma=False,
    )
```
